128 devices in a mesh: brick: 4 (over y), dom: 32 (over z, x, core).
Axes of the slice: x: 4, y: 4, z: 4, core: 2. Of those that a mesh axis runs over, the one named last changes fastest.
Arguments:
- strain: bfloat16 [162, 294912], P(None, ('brick', 'dom')), may hold values from -3 to 3
- strain_rate: bfloat16 [162, 294912], P(None, ('brick', 'dom')), may hold values from -3 to 3
- part_map: int32 [2, 294912], P(None, ('brick', 'dom')), may hold values from 0 to 127, as said below
- brick_map: int32 [2, 294912], P(None, ('brick', 'dom')), may hold values from 0 to 127, as said below
- connectivity: int32 [27, 294912], P(None, ('brick', 'dom')), may hold values from 0 to 29240, as said below
- density: float32 [294912], P(('brick', 'dom')), may hold values from 0.3 to 3
- weight_in: bfloat16 [128, 6], replicated, may hold values from -2.5 to 2.5
- bias_in: float32 [128], replicated, may hold values from -3 to 3
- weight_mid: bfloat16 [128, 128], replicated, may hold values from -0.5 to 0.5
- bias_mid: float32 [128], replicated, may hold values from -3 to 3
- weight_out: float32 [128], replicated, may hold values from -1.5 to 1.5
- grad_operator: bfloat16 [81, 162], replicated, may hold values from -0.5 to 0.5
Outputs:
- stress: bfloat16 [162, 294912], P(None, ('brick', 'dom'))
- stress_rate: bfloat16 [162, 294912], P(None, ('brick', 'dom'))
- nodal_force: float32 [3, 3742848], P(None, ('brick', 'dom'))
The draws below stay inside these ranges and needn't reach their ends.
Inputs may be any that keep to these rules, and one draw needn't show every extreme that they name: `part_map`: row 0 names the partition (device index over brick, then dom) that owns the element, row 1 its place among the elements that its device sends to that partition, below 32; no two elements of one device share a pair. Each device sends to 96 partitions: exactly 32 elements to half of them and 16 to the other half, and each partition receives exactly 2304 elements. `brick_map`: for element j of partition p, row 0 is the device of the brick layout that holds it and row 1 the place that this device's part_map gives it; every pair (device, place) that part_map sends to p appears exactly once among p's elements. `connectivity`: each partition's elements are the 9 x 256 x 1 quadratic hexahedra of a structured block, in an order drawn from the seed. Node (i, j, k), i < 19, j < 513, k < 3, has the number (i * 513 + j) * 3 + k, and row (u * 3 + w) * 3 + z of element (ex, ey) is node (2 ex + u, 2 ey + w, z). The plane i = 18 of a partition is the plane i = 0 of the next partition along dom in the same brick group.
All inputs are finite; a program needn't handle non-finite values.
Results may differ from the reference program's by a relative error of at most 0.0069.
Values may be sent and summed in bfloat16 or wider, within the bound.
A program may use at most 64 MiB of HBM per device.

```python
import math
import jax
import jax.numpy as jnp
import numpy as np
from jax import lax

WIDTH = 128
STRAIN = 6
GAUSS = 27
ELNODES = 27
SWEEPS = 3
ACROSS = 256
STRIP = 32
PARTITIONS = 128
ELEMS = 2304
ELEMS_ALL = 294912
CAPACITY = 32
GROUPS = 96
POINT_ROWS = 162
FORCE_ROWS = 81
PLANE = 1539
NODES = 29241
NODES_ALL = 3742848
N_BRICK = 4


def routing_plan(key):
    shifts = jax.random.permutation(jax.random.fold_in(key, 11), PARTITIONS)[:GROUPS].astype(jnp.int32)
    position = jnp.arange(ELEMS, dtype=jnp.int32)
    full_span = GROUPS // 2 * CAPACITY
    half_cap = CAPACITY // 2
    group_index = jnp.where(position < full_span, position // CAPACITY, GROUPS // 2 + (position - full_span) // half_cap)
    place_index = jnp.where(position < full_span, position % CAPACITY, (position - full_span) % half_cap)
    return (shifts, group_index.astype(jnp.int32), place_index.astype(jnp.int32))


def device_orders(key, salt):
    key_list = jax.random.split(jax.random.fold_in(key, salt), PARTITIONS)
    return jax.vmap(lambda single: jax.random.permutation(single, ELEMS))(key_list).astype(jnp.int32)


def draw_part_map(key, part):
    shifts, group_index, place_index = routing_plan(key)
    orders = device_orders(key, 12)
    source = jnp.arange(PARTITIONS, dtype=jnp.int32)[:, None]
    target = (source - shifts[group_index[orders]]) % PARTITIONS
    rank_index = place_index[orders]
    return jnp.stack([target.reshape(-1), rank_index.reshape(-1)]).astype(jnp.int32)


def draw_brick_map(key, part):
    shifts, group_index, place_index = routing_plan(key)
    orders = device_orders(key, 13)
    target = jnp.arange(PARTITIONS, dtype=jnp.int32)[:, None]
    source = (target + shifts[group_index[orders]]) % PARTITIONS
    rank_index = place_index[orders]
    return jnp.stack([source.reshape(-1), rank_index.reshape(-1)]).astype(jnp.int32)


def draw_connectivity(key, part):
    orders = device_orders(key, 14)
    along_index = orders // ACROSS
    across_index = orders % ACROSS
    corner = jnp.arange(ELNODES, dtype=jnp.int32)
    step_along = (corner // 9)[:, None, None]
    step_across = (corner // 3 % 3)[:, None, None]
    step_depth = (corner % 3)[:, None, None]
    node_ids = ((2 * along_index[None] + step_along) * (2 * ACROSS + 1) + 2 * across_index[None] + step_across) * 3 + step_depth
    return node_ids.reshape(ELNODES, PARTITIONS * ELEMS).astype(jnp.int32)


def level_of(key, dims, cuts, least, top_value):
    gain, own = 1.0, jax.random.fold_in(key, 6)
    for dim, shards_of in cuts:
        draws = jnp.exp(jax.random.uniform(jax.random.fold_in(own, dim), (shards_of,), jnp.float32, least / len(cuts), top_value / len(cuts)))
        gain = gain * jnp.repeat(draws, dims[dim] // shards_of).reshape([-1 if axis == dim else 1 for axis in range(len(dims))])
    return gain


def bell_draw(own_key, dims, scale, bound, cuts=(), kind=jnp.bfloat16):
    values = jax.random.normal(own_key, dims, jnp.float32) * scale
    if len(cuts) > 0:
        values = level_of(own_key, dims, cuts, -0.22, 0.18) * values
    return jnp.clip(values, min=-bound, max=bound).astype(kind)


def setup_inputs(seed: int = 0) -> dict:
    streams_of = jax.random.split(jax.random.key(seed), 13)
    return {
        "strain": bell_draw(streams_of[0], (POINT_ROWS, ELEMS_ALL), 0.5, 3.0, ((1, 128),)),
        "strain_rate": bell_draw(streams_of[1], (POINT_ROWS, ELEMS_ALL), 0.5, 3.0, ((1, 128),)),
        "part_map": draw_part_map(jax.random.fold_in(streams_of[12], 71), 0),
        "brick_map": draw_brick_map(jax.random.fold_in(streams_of[12], 71), 0),
        "connectivity": draw_connectivity(jax.random.fold_in(streams_of[12], 71), 0),
        "density": jnp.clip(jnp.exp(math.log(3.0) - 2.3025851 * jax.random.uniform(streams_of[5], (ELEMS_ALL,), jnp.float32) ** level_of(streams_of[5], (ELEMS_ALL,), ((0, 128),), -0.2, 0.2)), 0.3, 3.0),
        "weight_in": bell_draw(streams_of[6], (WIDTH, STRAIN), STRAIN ** -0.5, 2.5),
        "bias_in": bell_draw(streams_of[7], (WIDTH,), 0.5, 3.0, (), jnp.float32),
        "weight_mid": bell_draw(streams_of[8], (WIDTH, WIDTH), WIDTH ** -0.5, 0.5),
        "bias_mid": bell_draw(streams_of[9], (WIDTH,), 0.5, 3.0, (), jnp.float32),
        "weight_out": bell_draw(streams_of[10], (WIDTH,), (WIDTH // 8) ** -0.5, 1.5, (), jnp.float32),
        "grad_operator": bell_draw(streams_of[11], (FORCE_ROWS, POINT_ROWS), POINT_ROWS ** -0.5, 0.5),
    }


damping = 0.5


def mass_table():
    profile = np.array([[2.0, 1.0, 0.0], [1.0, 4.0, 1.0], [0.0, 1.0, 2.0]]) / 6.0
    table = profile[:, None, None, :, None, None] * profile[None, :, None, None, :, None] * profile[None, None, :, None, None, :]
    return table.reshape(27, 27)


def respond(strain_point, rate_point, weight_in, bias_in, weight_mid, bias_mid, weight_out):
    columns = strain_point.shape[1]
    act_one = jnp.tanh(jnp.dot(weight_in, strain_point, preferred_element_type=jnp.float32) + bias_in[:, None])
    slope_one = 1.0 - act_one * act_one
    tan_one = slope_one * jnp.dot(weight_in, rate_point, preferred_element_type=jnp.float32)
    joined = jnp.concatenate([act_one.astype(jnp.bfloat16), tan_one.astype(jnp.bfloat16)], axis=1)
    middle = jnp.dot(weight_mid, joined, preferred_element_type=jnp.float32)
    act_two = jnp.tanh(middle[:, :columns] + bias_mid[:, None])
    tan_two = middle[:, columns:]
    slope_two = 1.0 - act_two * act_two
    grad_two = weight_out[:, None] * slope_two
    curv_two = -2.0 * weight_out[:, None] * act_two * slope_two * tan_two
    joined_back = jnp.concatenate([grad_two.astype(jnp.bfloat16), curv_two.astype(jnp.bfloat16)], axis=1)
    backward = jnp.dot(weight_mid.T, joined_back, preferred_element_type=jnp.float32)
    back_one = backward[:, :columns]
    back_tan = backward[:, columns:]
    delta_one = slope_one * back_one
    delta_tan = slope_one * back_tan - 2.0 * act_one * tan_one * back_one
    joined_delta = jnp.concatenate([delta_one.astype(jnp.bfloat16), delta_tan.astype(jnp.bfloat16)], axis=1)
    result = jnp.dot(weight_in.T, joined_delta, preferred_element_type=jnp.float32)
    return result[:, :columns].astype(jnp.bfloat16), result[:, columns:].astype(jnp.bfloat16)


def pointwise(strain, strain_rate, weight_in, bias_in, weight_mid, bias_mid, weight_out):
    columns = strain.shape[1]
    points = (strain.reshape(GAUSS, STRAIN, columns), strain_rate.reshape(GAUSS, STRAIN, columns))

    def one_point(point_pair):
        return respond(point_pair[0], point_pair[1], weight_in, bias_in, weight_mid, bias_mid, weight_out)

    stress, stress_rate = lax.map(one_point, points)
    return stress.reshape(GAUSS * STRAIN, columns), stress_rate.reshape(GAUSS * STRAIN, columns)


def assemble(values, node_ids):
    height = values.shape[0]
    empty = jnp.zeros((height, NODES_ALL), jnp.float32)
    return empty.at[:, node_ids.reshape(-1)].add(values.reshape(height, -1))


def share(nodal):
    height = nodal.shape[0]
    strips = nodal.reshape(height, N_BRICK, STRIP, NODES)
    first_plane = strips[..., :PLANE]
    last_plane = strips[..., NODES - PLANE:]
    from_left = jnp.pad(last_plane[:, :, :-1], ((0, 0), (0, 0), (1, 0), (0, 0)))
    from_right = jnp.pad(first_plane[:, :, 1:], ((0, 0), (0, 0), (0, 1), (0, 0)))
    strips = strips.at[..., :PLANE].add(from_left)
    strips = strips.at[..., NODES - PLANE:].add(from_right)
    return strips.reshape(height, NODES_ALL)


def reference(strain, strain_rate, part_map, brick_map, connectivity, density, weight_in, bias_in, weight_mid, bias_mid, weight_out, grad_operator):
    stress, stress_rate = pointwise(strain, strain_rate, weight_in, bias_in, weight_mid, bias_mid, weight_out)
    elem_force = jnp.dot(grad_operator, stress, preferred_element_type=jnp.float32).astype(jnp.bfloat16)
    owner = (jnp.arange(ELEMS_ALL) // ELEMS).astype(jnp.int32)
    route_code = (owner * (PARTITIONS * CAPACITY) + part_map[0] * CAPACITY + part_map[1]).astype(jnp.int32)
    lookup = jnp.zeros((PARTITIONS * PARTITIONS * CAPACITY,), jnp.int32).at[route_code].set(jnp.arange(ELEMS_ALL).astype(jnp.int32))
    wanted = (brick_map[0] * (PARTITIONS * CAPACITY) + owner * CAPACITY + brick_map[1]).astype(jnp.int32)
    elem_part = elem_force[:, lookup[wanted]]
    node_ids = (connectivity + (owner * NODES)[None, :]).astype(jnp.int32)
    mass_ref = jnp.asarray(mass_table(), jnp.float32)
    nodal_load = share(assemble(elem_part.astype(jnp.float32).reshape(3, ELNODES, ELEMS_ALL), node_ids))
    weight = density[None, :] * jnp.diagonal(mass_ref)[:, None]
    diagonal = share(assemble(weight[None], node_ids))
    nodal_force = damping * nodal_load / diagonal
    for iteration in range(SWEEPS - 1):
        gathered = nodal_force[:, node_ids]
        applied = jnp.einsum("ab,dbe->dae", mass_ref, gathered, precision=lax.Precision.HIGHEST) * density[None, None, :]
        nodal_force = nodal_force + damping * (nodal_load - share(assemble(applied, node_ids))) / diagonal
    return stress, stress_rate, nodal_force
```

```python
import functools

import jax
import jax.numpy as jnp
import numpy as np
from jax import lax
from jax.experimental import pallas as pl
from jax.experimental.pallas import tpu as pltpu
from jax.sharding import PartitionSpec as P

BF = jnp.bfloat16
F32 = jnp.float32
G = 27
VAR = 0

def dot(a,b): return jnp.dot(a,b,preferred_element_type=F32)
def dot_nt(a,b): return lax.dot_general(a,b,(((1,),(1,)),((),())),preferred_element_type=F32)

def consts():
    selx=np.zeros((432,162),np.float32); selv=np.zeros((432,162),np.float32); ones=np.zeros((432,1),np.float32)
    selo=np.zeros((162,216),np.float32)
    for g in range(27):
        for c in range(6):
            selx[g*16+c,g*6+c]=1; selv[g*16+8+c,g*6+c]=1; selo[g*6+c,g*8+c]=1
        for r in (6,7,14): ones[g*16+r]=1
    return selx,selv,ones,selo

def prep(weight_in,bias_in,weight_mid,bias_mid,weight_out,grad_operator):
    rp=lambda a: lax.reduce_precision(a,8,7)
    hi=rp(bias_in); r=bias_in-hi; lo=rp(r); lo2=(r-lo).astype(BF); hi=hi.astype(BF); lo=lo.astype(BF)
    z=lambda a,b: jnp.zeros((a,b),BF)
    top=jnp.concatenate([weight_in,hi[:,None],lo[:,None],z(128,6),lo2[:,None],z(128,1)],1)
    bot=jnp.concatenate([z(128,8),weight_in,z(128,2)],1)
    win2=jnp.concatenate([top,bot],0)
    wback=weight_mid.T
    wt=jnp.pad(weight_in.T,((0,2),(0,0)))
    selx,selv,ones,selo=consts()
    selo=jnp.asarray(selo,BF)
    g3=jnp.pad(grad_operator.reshape(3,27,162),((0,0),(0,5),(0,0))).reshape(96,162)
    gsel=dot(g3,selo).astype(BF)
    so=jnp.concatenate([selo,gsel,jnp.zeros((14,216),BF)],0)
    return (jnp.asarray(selx,BF),jnp.asarray(selv,BF),jnp.asarray(np.tile(ones,(1,128)),F32),win2,weight_mid,jnp.stack([bias_mid,weight_out],1),wback,wt,so)

def kernelA(C,U,steps,x_ref,v_ref,pm_ref,selx,selv,ones,win2,wmid,bmid,wback,wt,so,s_ref,r_ref,send_ref,x16,o1,o2,fs):
    step=pl.program_id(0)
    xx=dot(selx[...],x_ref[...])+dot(selv[...],v_ref[...])
    x16[...]=(xx+ones[:,0:1]).astype(BF)
    def one(g):
        xg=x16[pl.ds(pl.multiple_of(g*16,16),16),:]
        h=dot(win2[...],xg)
        act=jnp.tanh(h[:128]); slope=1.0-act*act; tan=slope*h[128:]
        if VAR&1:
            mm=dot(wmid[...],jnp.concatenate([act.astype(BF),tan.astype(BF)],1)); m1=mm[:,:C]; m2=mm[:,C:]
        else:
            m1=dot(wmid[...],act.astype(BF)); m2=dot(wmid[...],tan.astype(BF))
        act2=jnp.tanh(m1+bmid[:,0:1]); s2=bmid[:,1:2]*(1.0-act2*act2)
        b1=dot(wback[...],s2.astype(BF)); b2=dot(wback[...],(act2*s2*m2).astype(BF))
        d1=(slope*b1).astype(BF); d2=(slope*b2+act*tan*b1).astype(BF)
        gg=pl.ds(pl.multiple_of(g*8,8),8)
        o1[gg,:]=dot(wt[...],d1)
        o2[gg,:]=dot(wt[...],d2)*-2.0
    def body(i,c):
        for u in range(U): one(i*U+u)
        return c
    lax.fori_loop(0,G//U,body,0)
    o1b=o1[...].astype(BF); o2b=o2[...].astype(BF)
    so1=so[0:162,:]
    s_ref[...]=dot(so1,o1b).astype(BF)
    r_ref[...]=dot(so1,o2b).astype(BF)
    fcol=dot(so[162:258,:],o1b).astype(BF)
    fs[:,pl.ds(pl.multiple_of(step*C,128),C)]=fcol
    @pl.when(step==steps-1)
    def _():
        n=fs.shape[1]
        p=pm_ref[0:1,:]; r=pm_ref[1:2,:]
        hi=p*8+r//4; lo=r%4
        F=fs[...].astype(F32)
        mf=[]
        for d in range(3):
            for l in range(4):
                mf.append(jnp.where(lo==l,F[d*32:(d+1)*32],0.0).astype(BF))
        mf=jnp.concatenate(mf,0)
        for blk in range(2):
            io=lax.broadcasted_iota(jnp.int32,(512,n),0)+blk*512
            oh=jnp.where(io==hi,1.0,0.0).astype(BF)
            out=dot_nt(oh,mf).astype(BF)
            for d in range(3):
                send_ref[blk*64:(blk+1)*64,d]=out[:,d*128:(d+1)*128].reshape(64,8,128)

def callA(strain,rate,pm,pr,C=256,U=3):
    n=strain.shape[1]; steps=n//C
    full=lambda a: pl.BlockSpec(a.shape,lambda i:(0,)*a.ndim)
    col=pl.BlockSpec((162,C),lambda i:(0,i))
    return pl.pallas_call(functools.partial(kernelA,C,U,steps),
        out_shape=(jax.ShapeDtypeStruct((162,n),BF),jax.ShapeDtypeStruct((162,n),BF),jax.ShapeDtypeStruct((128,3,8,128),BF)),
        grid=(steps,),
        in_specs=[col,col,full(pm)]+[full(a) for a in pr],
        out_specs=(col,col,pl.BlockSpec((128,3,8,128),lambda i:(0,0,0,0))),
        scratch_shapes=[pltpu.VMEM((432,C),BF),pltpu.VMEM((216,C),F32),pltpu.VMEM((216,C),F32),pltpu.VMEM((96,n),BF)],
        compiler_params=pltpu.CompilerParams(vmem_limit_bytes=48<<20),
        name="pointwise_send",
        cost_estimate=pl.CostEstimate(flops=16*10**9,bytes_accessed=4*10**6,transcendentals=16*10**6),
    )(strain,rate,pm,*pr)

def kernelC(r_ref,bm_ref,conn_ref,dens_ref,eg_ref):
    n=2304
    c0=conn_ref[0:1,:].astype(F32)
    nr=jnp.floor((c0+0.5)*(1.0/3.0))
    ix=jnp.floor((nr+0.5)*(1.0/513.0))
    ey=(nr-ix*513.0)*0.5
    up=jnp.where(ey>=128.0,1.0,0.0)
    ghi=(ix+up).astype(jnp.int32); glo=(ey-128.0*up).astype(jnp.int32)
    dens=dens_ref[...]
    d1=dens.astype(BF).astype(F32); e=dens-d1
    d2=e.astype(BF).astype(F32); d3=e-d2
    v=jnp.concatenate([bm_ref[0:1,:].astype(F32),bm_ref[1:2,:].astype(F32),d1,d2,d3,jnp.zeros((3,n),F32)],0)
    vm=jnp.concatenate([jnp.where(ghi==h,v,0.0) for h in range(18)],0).astype(BF)
    ohl=jnp.where(lax.broadcasted_iota(jnp.int32,(128,n),0)==glo,1.0,0.0).astype(BF)
    o=dot_nt(vm,ohl)
    vs=jnp.concatenate([o[h*8:(h+1)*8,:] for h in range(18)],1)
    rr=vs[1:2,:]; rhi=jnp.floor(rr*0.25)
    hi=(vs[0:1,:]*8.0+rhi).astype(jnp.int32); lo=(rr-4.0*rhi).astype(jnp.int32)
    R=jnp.concatenate([r_ref[:,d].reshape(1024,128) for d in range(3)],1)
    N=768
    row=lax.broadcasted_iota(jnp.int32,(32,N),0)
    for k in range(n//N):
        sl=slice(k*N,(k+1)*N)
        oh=jnp.where(lax.broadcasted_iota(jnp.int32,(1024,N),0)==hi[:,sl],1.0,0.0).astype(BF)
        T=lax.dot_general(R,oh,(((0,),(0,)),((),())),preferred_element_type=F32)
        for d in range(3):
            acc=jnp.where(row==27,vs[2+d:3+d,sl],0.0)
            for l in range(4):
                acc=acc+jnp.where(lo[:,sl]==l,T[d*128+l*32:d*128+(l+1)*32],0.0)
            eg_ref[d*32:(d+1)*32,sl]=acc.astype(BF)

def callC(R,bm,conn,dens):
    n=2304
    full=lambda a: pl.BlockSpec(a.shape,lambda i:(0,)*a.ndim)
    return pl.pallas_call(kernelC,grid=(1,),out_shape=jax.ShapeDtypeStruct((96,n),BF),
      in_specs=[full(R),full(bm),pl.BlockSpec((8,n),lambda i:(0,0)),full(dens)],
      out_specs=pl.BlockSpec((96,n),lambda i:(0,0)),
      compiler_params=pltpu.CompilerParams(vmem_limit_bytes=48<<20),name="take")(R,bm,conn,dens)

def fe_consts():
    m=np.array([[2,1,0],[1,4,1],[0,1,2]],np.float64)
    def rowof(u,w,z,d): return (u*3+w)*16+z*3+d
    A=np.zeros((144,144)); S=np.zeros((144,96)); dg=np.ones((144,1)); Q=np.zeros((216,144))
    for u in range(3):
     for w in range(3):
      for z in range(3):
       for d in range(3):
        r=rowof(u,w,z,d)
        S[r,d*32+(u*3+w)*3+z]=1
        dg[r]=m[u,u]*m[w,w]*m[z,z]
        Q[((u*3+w)*3+z)*8+d,r]=1
        for u2 in range(3):
         for w2 in range(3):
          for z2 in range(3):
            A[r,rowof(u2,w2,z2,d)]=m[u,u2]*m[w,w2]*m[z,z2]
    nn=np.arange(768); j=nn//3; z=nn%3; src=((j%2)*3+z)*128+j//2
    return A,S,np.tile(dg,(1,128)),Q,src[None,:].astype(np.int32)

def kernelE(L,O,Rt,A,S,dg,Q,src,out_ref):
    ext=jnp.concatenate([L[...],O[...],Rt[...]],1)
    dens=(ext[27:28].astype(F32)+ext[59:60].astype(F32)+ext[91:92].astype(F32))*(1.0/216.0)
    def shl(x):
        n=x.shape[1]; y=pltpu.roll(x,n-1,1)
        i=lax.broadcasted_iota(jnp.int32,(1,n),1)&255
        return jnp.where(i==255,0.0,y)
    def shr(x):
        n=x.shape[1]; y=pltpu.roll(x,1,1)
        i=lax.broadcasted_iota(jnp.int32,(1,n),1)&255
        return jnp.where(i==0,0.0,y)
    def assemble(h):
        g=[h[16*q:16*q+16] for q in range(9)]
        for u in range(3):
            a0,a2=g[u*3],g[u*3+2]
            g[u*3]=a0+shr(a2); g[u*3+2]=a2+shl(a0)
        z=jnp.zeros((16,256),F32); n=h.shape[1]
        for w in range(3):
            b0,b2=g[w],g[6+w]
            g[w]=b0+jnp.concatenate([z,b2[:,:n-256]],1)
            g[6+w]=b2+jnp.concatenate([b0[:,256:],z],1)
        return jnp.concatenate(g,0)
    load=assemble(dot(S[...],ext))
    diag=assemble(dg[:,0:1]*dens)
    hinv=0.5/jnp.where(diag>0.0,diag,1.0)
    c=lambda x: x[:,256:x.shape[1]-256]
    load=c(load); hinv=c(hinv); dens=c(dens)
    f=load*hinv
    for it in range(2):
        fh=f.astype(BF); fl=(f-fh.astype(F32)).astype(BF)
        h=(dot(A[...],fh)+dot(A[...],fl))*dens
        s=assemble(h)
        f=c(f+(load-s)*hinv)
        load=c(load); hinv=c(hinv); dens=c(dens)
    fh=f.astype(BF); fl=(f-fh.astype(F32)).astype(BF)
    parts=[dot(Q[...],fh),dot(Q[...],fl)]
    P=jnp.where(lax.broadcasted_iota(jnp.int32,(768,768),0)==src[...],1.0,0.0).astype(BF)
    lhs=[]
    for half in range(2):
        for p in parts:
            rows=[]
            for i in range(19):
                u,ex=(i%2,i//2) if i<18 else (2,8)
                b=ex*256+half*128
                rows.append(jnp.concatenate([p[((u*3+w)*3+z)*8:((u*3+w)*3+z)*8+8,b:b+128] for w in range(2) for z in range(3)],1))
            lhs.append(jnp.concatenate(rows,0))
    Y=dot(jnp.concatenate(lhs,0).astype(BF),P)
    fs=parts[0]+parts[1]
    for i in range(19):
        u,ex=(i%2,i//2) if i<18 else (2,8)
        r=slice(8*i,8*i+8)
        h0=Y[0:152][r]+Y[152:304][r]; h1=Y[304:456][r]+Y[456:608][r]
        last=[fs[((u*3+2)*3+z)*8:((u*3+2)*3+z)*8+8,ex*256+255:ex*256+256] for z in range(3)]
        val=jnp.concatenate([h0,h1]+last,1)
        out_ref[:,i*1539:(i+1)*1539]=val[0:3]

def callE(L,O,Rt):
    A,S,dg,Q,src=fe_consts()
    ops=[L,O,Rt,jnp.asarray(A,BF),jnp.asarray(S,BF),jnp.asarray(dg,F32),jnp.asarray(Q,BF),jnp.asarray(src)]
    full=lambda a: pl.BlockSpec(a.shape,lambda i:(0,)*a.ndim)
    return pl.pallas_call(kernelE,grid=(1,),out_shape=jax.ShapeDtypeStruct((3,29241),F32),
      in_specs=[full(a) for a in ops],out_specs=pl.BlockSpec((3,29241),lambda i:(0,0)),
      compiler_params=pltpu.CompilerParams(vmem_limit_bytes=48<<20),name="project")(*ops)


def per_device(strain, strain_rate, part_map, brick_map, connectivity, density, *weights):
    stress, stress_rate, send = callA(strain, strain_rate, part_map, prep(*weights), 2304, 3)
    recv = lax.all_to_all(send, ("brick", "dom"), split_axis=0, concat_axis=0, tiled=True)
    grid = callC(recv, brick_map, connectivity, density.reshape(1, -1))
    count = lax.axis_size("dom")
    left = lax.ppermute(grid[:, 1536:], "dom", [(i, i + 1) for i in range(count - 1)])
    right = lax.ppermute(grid[:, :768], "dom", [(i + 1, i) for i in range(count - 1)])
    return stress, stress_rate, callE(left, grid, right)


def solution(mesh):
    split = P(None, ("brick", "dom"))
    return jax.shard_map(
        per_device,
        mesh=mesh,
        in_specs=(split,) * 5 + (P(("brick", "dom")),) + (P(),) * 6,
        out_specs=(split,) * 3,
        check_vma=False,
    )
```

```python
import functools

import jax
import jax.numpy as jnp
import numpy as np
from jax import lax
from jax.experimental import pallas as pl
from jax.experimental.pallas import tpu as pltpu
from jax.sharding import PartitionSpec as P

BF=jnp.bfloat16; F32=jnp.float32
def dot(a,b): return jnp.dot(a,b,preferred_element_type=F32)
def dot_nt(a,b): return lax.dot_general(a,b,(((1,),(1,)),((),())),preferred_element_type=F32)
MESH=pl.DeviceIdType.MESH
EARLY=17
U=1
REMOTE=True


def iota(shape, axis):
    return lax.broadcasted_iota(jnp.int32, shape, axis)


def ones_where(mask):
    return jnp.where(mask, 1.0, 0.0).astype(BF)


def pointwise_kernel(x_ref, v_ref, pm_ref, win_ref, bin_ref, wmid_ref, bmid_ref, wout_ref, grad_ref, s_ref, r_ref, recv_ref,
                     x16, oo, bias, win2, wmid2, wback2, wt2, send, send_sem, recv_sem, own_sem):
    n = x_ref.shape[1]
    if REMOTE:
        nb, nd = lax.axis_size("brick"), lax.axis_size("dom")
        devices = nb * nd
        b, d = lax.axis_index("brick"), lax.axis_index("dom")
        me = b * nd + d
        barrier = pltpu.get_barrier_semaphore()

        def greet(k, carry):
            t = lax.rem(me + k, devices)
            pl.semaphore_signal(barrier, inc=1, device_id=(lax.div(t, nd), lax.rem(t, nd)), device_id_type=MESH)
            return carry

        lax.fori_loop(1, devices, greet, 0)

    win = win_ref[...]
    e16 = lambda k: ones_where(iota((6, 16), 1) == iota((6, 16), 0) + k)
    win2[0:128] = dot(win, e16(0)).astype(BF)
    win2[128:256] = dot(win, e16(8)).astype(BF)
    wmid = wmid_ref[...]
    zero = jnp.zeros((128, 128), BF)
    wmid2[...] = jnp.concatenate([jnp.concatenate([wmid, zero], 1), jnp.concatenate([zero, wmid], 1)], 0)
    back = wmid.astype(F32).T.astype(BF)
    wback2[...] = jnp.concatenate([jnp.concatenate([back, zero], 1), jnp.concatenate([zero, back], 1)], 0)
    e = lambda k: ones_where(iota((16, 6), 0) == iota((16, 6), 1) + k)
    wt2[...] = jnp.concatenate([dot_nt(e(0), win).astype(BF), (-2.0 * dot_nt(e(8), win)).astype(BF)], 1)
    for k, row in enumerate((bin_ref, bmid_ref, wout_ref)):
        bias[k] = jnp.broadcast_to(row[...], (128, 128)).T

    r, c = iota((432, 162), 0), iota((432, 162), 1)
    first, place = lax.shift_right_logical(r, 4) * 6, r & 15
    selx = ones_where((c == first + place) & (place < 6))
    selv = ones_where((c == first + place - 8) & (place >= 8) & (place < 14))
    for k in range(0, n, 768):
        sl = slice(k, k + 768)
        x16[:, sl] = (dot(selx, x_ref[:, sl]) + dot(selv, v_ref[:, sl])).astype(BF)

    def column(k):
        return jnp.concatenate([bias[k]] * (n // 128), 1)

    def group(g):
        return pl.ds(pl.multiple_of(g * 16, 16), 16)

    def both(g):
        h = dot(win2[...], x16[group(g), :])
        act = jnp.tanh(h[:128] + column(0))
        slope = 1.0 - act * act
        tan = slope * h[128:]
        m = dot(wmid2[...], jnp.concatenate([act.astype(BF), tan.astype(BF)], 0))
        act2 = jnp.tanh(m[:128] + column(1))
        grad = column(2) * (1.0 - act2 * act2)
        bk = dot(wback2[...], jnp.concatenate([grad.astype(BF), (act2 * grad * m[128:]).astype(BF)], 0))
        b1 = bk[:128]
        d2 = slope * bk[128:] + act * tan * b1
        oo[group(g), :] = dot(wt2[...], jnp.concatenate([(slope * b1).astype(BF), d2.astype(BF)], 0))

    def value(g):
        act = jnp.tanh(dot(win2[0:128], x16[group(g), :]) + column(0))
        act2 = jnp.tanh(dot(wmid2[0:128, 0:128], act.astype(BF)) + column(1))
        grad = column(2) * (1.0 - act2 * act2)
        b1 = dot(wback2[0:128, 0:128], grad.astype(BF))
        oo[group(g), :] = dot(wt2[:, 0:128], ((1.0 - act * act) * b1).astype(BF))

    def run(body, low, high):
        def step(i, carry):
            for u in range(U):
                body(low + i * U + u)
            return carry
        lax.fori_loop(0, (high - low) // U, step, 0)

    run(both, 0, EARLY)
    if EARLY < 27: run(value, EARLY, 27)

    r, c = iota((162, 432), 0), iota((162, 432), 1)
    first, place = lax.shift_right_logical(c, 4) * 6, c & 15
    pick_s = ones_where((r == first + place) & (place < 6))
    pick_r = ones_where((r == first + place - 8) & (place >= 8) & (place < 14))
    r, c = iota((96, 81), 0), iota((96, 81), 1)
    lane = r & 31
    grad_op = dot(ones_where((c == lax.shift_right_logical(r, 5) * 27 + lane) & (lane < 27)), grad_ref[...]).astype(BF)
    parts = []
    for k in range(0, n, 768):
        sl = slice(k, k + 768)
        stress = dot(pick_s, oo[:, sl].astype(BF)).astype(BF)
        s_ref[:, sl] = stress
        parts.append(dot(grad_op, stress).astype(BF).astype(F32))
    force = jnp.concatenate(parts, 1)
    place = pm_ref[1:2, :]
    high = pm_ref[0:1, :] * 8 + lax.shift_right_logical(place, 2)
    low = place & 3
    masked = jnp.concatenate(
        [jnp.where(low == l, force[a * 32:(a + 1) * 32], 0.0).astype(BF) for a in range(3) for l in range(4)], 0)
    for k in range(2):
        onehot = ones_where(iota((512, n), 0) + k * 512 == high)
        out = dot_nt(onehot, masked).astype(BF)
        for a in range(3):
            send[k * 64:(k + 1) * 64, a] = out[:, a * 128:(a + 1) * 128].reshape(64, 8, 128)

    if REMOTE:
        pl.semaphore_wait(barrier, devices - 1)
        own = pltpu.make_async_copy(send.at[me], recv_ref.at[me], own_sem)
        own.start()

        def push(k, carry):
            t = lax.rem(me + k, devices)
            pltpu.make_async_remote_copy(
                src_ref=send.at[t], dst_ref=recv_ref.at[me], send_sem=send_sem, recv_sem=recv_sem,
                device_id=(lax.div(t, nd), lax.rem(t, nd)), device_id_type=MESH).start()
            return carry

        lax.fori_loop(1, devices, push, 0)

    if EARLY < 27: run(both, EARLY, 27)
    for k in range(0, n, 768):
        sl = slice(k, k + 768)
        r_ref[:, sl] = dot(pick_r, oo[:, sl].astype(BF)).astype(BF)

    if REMOTE:
        own.wait()
        every = pltpu.make_async_remote_copy(
            src_ref=send.at[pl.ds(0, devices - 1)], dst_ref=recv_ref.at[pl.ds(0, devices - 1)],
            send_sem=send_sem, recv_sem=recv_sem, device_id=(b, d), device_id_type=MESH)
        every.wait_send()
        every.wait_recv()
    else:
        recv_ref[...] = send[...]


def pointwise(strain, rate, part_map, weight_in, bias_in, weight_mid, bias_mid, weight_out, grad_operator):
    n = strain.shape[1]
    row = lambda a: a.reshape(1, 128)
    out = jax.ShapeDtypeStruct((162, n), BF)
    vmem = pl.BlockSpec(memory_space=pltpu.VMEM)
    return pl.pallas_call(
        pointwise_kernel,
        out_shape=(out, out, jax.ShapeDtypeStruct((128, 3, 8, 128), BF)),
        in_specs=[vmem] * 9,
        out_specs=(vmem,) * 3,
        scratch_shapes=[
            pltpu.VMEM((432, n), BF), pltpu.VMEM((432, n), F32), pltpu.VMEM((3, 128, 128), F32), pltpu.VMEM((256, 16), BF),
            pltpu.VMEM((256, 256), BF), pltpu.VMEM((256, 256), BF), pltpu.VMEM((16, 256), BF), pltpu.VMEM((128, 3, 8, 128), BF),
            pltpu.SemaphoreType.DMA, pltpu.SemaphoreType.DMA, pltpu.SemaphoreType.DMA,
        ],
        compiler_params=pltpu.CompilerParams(vmem_limit_bytes=60 << 20, **(dict(collective_id=0, has_side_effects=True) if REMOTE else {})),
        name="pointwise",
    )(strain, rate, part_map, weight_in, row(bias_in), weight_mid, row(bias_mid), row(weight_out), grad_operator)

def kernelC(r_ref,bm_ref,conn_ref,dens_ref,eg_ref):
    n=2304
    c0=conn_ref[0:1,:].astype(F32)
    nr=jnp.floor((c0+0.5)*(1.0/3.0))
    ix=jnp.floor((nr+0.5)*(1.0/513.0))
    ey=(nr-ix*513.0)*0.5
    up=jnp.where(ey>=128.0,1.0,0.0)
    ghi=(ix+up).astype(jnp.int32); glo=(ey-128.0*up).astype(jnp.int32)
    dens=dens_ref[...]
    d1=dens.astype(BF).astype(F32); e=dens-d1
    d2=e.astype(BF).astype(F32); d3=e-d2
    v=jnp.concatenate([bm_ref[0:1,:].astype(F32),bm_ref[1:2,:].astype(F32),d1,d2,d3,jnp.zeros((3,n),F32)],0)
    vm=jnp.concatenate([jnp.where(ghi==h,v,0.0) for h in range(18)],0).astype(BF)
    ohl=jnp.where(lax.broadcasted_iota(jnp.int32,(128,n),0)==glo,1.0,0.0).astype(BF)
    o=dot_nt(vm,ohl)
    vs=jnp.concatenate([o[h*8:(h+1)*8,:] for h in range(18)],1)
    rr=vs[1:2,:]; rhi=jnp.floor(rr*0.25)
    hi=(vs[0:1,:]*8.0+rhi).astype(jnp.int32); lo=(rr-4.0*rhi).astype(jnp.int32)
    R=jnp.concatenate([r_ref[:,d].reshape(1024,128) for d in range(3)],1)
    N=768
    row=lax.broadcasted_iota(jnp.int32,(32,N),0)
    for k in range(n//N):
        sl=slice(k*N,(k+1)*N)
        oh=jnp.where(lax.broadcasted_iota(jnp.int32,(1024,N),0)==hi[:,sl],1.0,0.0).astype(BF)
        T=lax.dot_general(R,oh,(((0,),(0,)),((),())),preferred_element_type=F32)
        for d in range(3):
            acc=jnp.where(row==27,vs[2+d:3+d,sl],0.0)
            for l in range(4):
                acc=acc+jnp.where(lo[:,sl]==l,T[d*128+l*32:d*128+(l+1)*32],0.0)
            eg_ref[d*32:(d+1)*32,sl]=acc.astype(BF)

def callC(R,bm,conn,dens):
    n=2304
    full=lambda a: pl.BlockSpec(a.shape,lambda i:(0,)*a.ndim)
    return pl.pallas_call(kernelC,grid=(1,),out_shape=jax.ShapeDtypeStruct((96,n),BF),
      in_specs=[full(R),full(bm),pl.BlockSpec((8,n),lambda i:(0,0)),full(dens)],
      out_specs=pl.BlockSpec((96,n),lambda i:(0,0)),
      compiler_params=pltpu.CompilerParams(vmem_limit_bytes=60<<20),name="take")(R,bm,conn,dens)

def fe_consts():
    m=np.array([[2,1,0],[1,4,1],[0,1,2]],np.float64)
    def rowof(u,w,z,d): return (u*3+w)*16+z*3+d
    A=np.zeros((144,144)); S=np.zeros((144,96)); dg=np.ones((144,1)); Q=np.zeros((216,144))
    for u in range(3):
     for w in range(3):
      for z in range(3):
       for d in range(3):
        r=rowof(u,w,z,d)
        S[r,d*32+(u*3+w)*3+z]=1
        dg[r]=m[u,u]*m[w,w]*m[z,z]
        Q[((u*3+w)*3+z)*8+d,r]=1
        for u2 in range(3):
         for w2 in range(3):
          for z2 in range(3):
            A[r,rowof(u2,w2,z2,d)]=m[u,u2]*m[w,w2]*m[z,z2]
    nn=np.arange(768); j=nn//3; z=nn%3; src=((j%2)*3+z)*128+j//2
    return A,S,np.tile(dg,(1,128)),Q,src[None,:].astype(np.int32)

def kernelE(L,O,Rt,A,S,dg,Q,src,out_ref):
    ext=jnp.concatenate([L[...],O[...],Rt[...]],1)
    dens=(ext[27:28].astype(F32)+ext[59:60].astype(F32)+ext[91:92].astype(F32))*(1.0/216.0)
    def shl(x):
        n=x.shape[1]; y=pltpu.roll(x,n-1,1)
        i=lax.broadcasted_iota(jnp.int32,(1,n),1)&255
        return jnp.where(i==255,0.0,y)
    def shr(x):
        n=x.shape[1]; y=pltpu.roll(x,1,1)
        i=lax.broadcasted_iota(jnp.int32,(1,n),1)&255
        return jnp.where(i==0,0.0,y)
    def assemble(h):
        g=[h[16*q:16*q+16] for q in range(9)]
        for u in range(3):
            a0,a2=g[u*3],g[u*3+2]
            g[u*3]=a0+shr(a2); g[u*3+2]=a2+shl(a0)
        z=jnp.zeros((16,256),F32); n=h.shape[1]
        for w in range(3):
            b0,b2=g[w],g[6+w]
            g[w]=b0+jnp.concatenate([z,b2[:,:n-256]],1)
            g[6+w]=b2+jnp.concatenate([b0[:,256:],z],1)
        return jnp.concatenate(g,0)
    load=assemble(dot(S[...],ext))
    diag=assemble(dg[:,0:1]*dens)
    hinv=0.5/jnp.where(diag>0.0,diag,1.0)
    c=lambda x: x[:,256:x.shape[1]-256]
    load=c(load); hinv=c(hinv); dens=c(dens)
    f=load*hinv
    for it in range(2):
        fh=f.astype(BF); fl=(f-fh.astype(F32)).astype(BF)
        h=(dot(A[...],fh)+dot(A[...],fl))*dens
        s=assemble(h)
        f=c(f+(load-s)*hinv)
        load=c(load); hinv=c(hinv); dens=c(dens)
    fh=f.astype(BF); fl=(f-fh.astype(F32)).astype(BF)
    parts=[dot(Q[...],fh),dot(Q[...],fl)]
    P=jnp.where(lax.broadcasted_iota(jnp.int32,(768,768),0)==src[...],1.0,0.0).astype(BF)
    lhs=[]
    for half in range(2):
        for p in parts:
            rows=[]
            for i in range(19):
                u,ex=(i%2,i//2) if i<18 else (2,8)
                b=ex*256+half*128
                rows.append(jnp.concatenate([p[((u*3+w)*3+z)*8:((u*3+w)*3+z)*8+8,b:b+128] for w in range(2) for z in range(3)],1))
            lhs.append(jnp.concatenate(rows,0))
    Y=dot(jnp.concatenate(lhs,0).astype(BF),P)
    fs=parts[0]+parts[1]
    for i in range(19):
        u,ex=(i%2,i//2) if i<18 else (2,8)
        r=slice(8*i,8*i+8)
        h0=Y[0:152][r]+Y[152:304][r]; h1=Y[304:456][r]+Y[456:608][r]
        last=[fs[((u*3+2)*3+z)*8:((u*3+2)*3+z)*8+8,ex*256+255:ex*256+256] for z in range(3)]
        val=jnp.concatenate([h0,h1]+last,1)
        out_ref[:,i*1539:(i+1)*1539]=val[0:3]

def callE(L,O,Rt):
    A,S,dg,Q,src=fe_consts()
    ops=[L,O,Rt,jnp.asarray(A,BF),jnp.asarray(S,BF),jnp.asarray(dg,F32),jnp.asarray(Q,BF),jnp.asarray(src)]
    full=lambda a: pl.BlockSpec(a.shape,lambda i:(0,)*a.ndim)
    return pl.pallas_call(kernelE,grid=(1,),out_shape=jax.ShapeDtypeStruct((3,29241),F32),
      in_specs=[full(a) for a in ops],out_specs=pl.BlockSpec((3,29241),lambda i:(0,0)),
      compiler_params=pltpu.CompilerParams(vmem_limit_bytes=60<<20),name="project")(*ops)


def per_device(strain, strain_rate, part_map, brick_map, connectivity, density, *weights):
    stress, stress_rate, recv = pointwise(strain, strain_rate, part_map, *weights)
    grid = callC(recv, brick_map, connectivity, density.reshape(1, -1))
    count = lax.axis_size("dom")
    left = lax.ppermute(grid[:, 1536:], "dom", [(i, i + 1) for i in range(count - 1)])
    right = lax.ppermute(grid[:, :768], "dom", [(i + 1, i) for i in range(count - 1)])
    return stress, stress_rate, callE(left, grid, right)


def solution(mesh):
    split = P(None, ("brick", "dom"))
    return jax.shard_map(
        per_device,
        mesh=mesh,
        in_specs=(split,) * 5 + (P(("brick", "dom")),) + (P(),) * 6,
        out_specs=(split,) * 3,
        check_vma=False,
    )
```

```python
import functools

import jax
import jax.numpy as jnp
import numpy as np
from jax import lax
from jax.experimental import pallas as pl
from jax.experimental.pallas import tpu as pltpu
from jax.sharding import PartitionSpec as P

BF=jnp.bfloat16; F32=jnp.float32
def dot(a,b): return jnp.dot(a,b,preferred_element_type=F32)
def dot_nt(a,b): return lax.dot_general(a,b,(((1,),(1,)),((),())),preferred_element_type=F32)
MESH=pl.DeviceIdType.MESH
EARLY=17
U=1
REMOTE=True


def iota(shape, axis):
    return lax.broadcasted_iota(jnp.int32, shape, axis)


def ones_where(mask):
    return jnp.where(mask, 1.0, 0.0).astype(BF)


def pointwise_kernel(x_ref, v_ref, pm_ref, bm_ref, conn_ref, dens_ref, win_ref, bin_ref, wmid_ref, bmid_ref, wout_ref, grad_ref,
                     s_out, r_out, grid_ref, left_ref, right_ref, s_ref, r_ref, x16, oo, bias, win2, wmid2, wback2, wt2, send,
                     recv_ref, pick, send_sem, recv_sem, own_sem, s_sem, r_sem, left_send, left_recv, right_send, right_recv):
    n = x_ref.shape[1]
    if REMOTE:
        nb, nd = lax.axis_size("brick"), lax.axis_size("dom")
        devices = nb * nd
        b, d = lax.axis_index("brick"), lax.axis_index("dom")
        me = b * nd + d
        barrier = pltpu.get_barrier_semaphore()

        def greet(k, carry):
            t = lax.rem(me + k, devices)
            pl.semaphore_signal(barrier, inc=1, device_id=(lax.div(t, nd), lax.rem(t, nd)), device_id_type=MESH)
            return carry

        lax.fori_loop(1, devices, greet, 0)

    win = win_ref[...].astype(F32).T.astype(BF)
    e16 = lambda k: ones_where(iota((6, 16), 1) == iota((6, 16), 0) + k)
    win2[0:128] = dot(win, e16(0)).astype(BF)
    win2[128:256] = dot(win, e16(8)).astype(BF)
    wmid = wmid_ref[...]
    zero = jnp.zeros((128, 128), BF)
    wmid2[...] = jnp.concatenate([jnp.concatenate([wmid, zero], 1), jnp.concatenate([zero, wmid], 1)], 0)
    back = wmid.astype(F32).T.astype(BF)
    wback2[...] = jnp.concatenate([jnp.concatenate([back, zero], 1), jnp.concatenate([zero, back], 1)], 0)
    e = lambda k: ones_where(iota((16, 6), 0) == iota((16, 6), 1) + k)
    wt2[...] = jnp.concatenate([dot_nt(e(0), win).astype(BF), (-2.0 * dot_nt(e(8), win)).astype(BF)], 1)
    for k, row in enumerate((bin_ref, bmid_ref, wout_ref)):
        bias[k] = jnp.broadcast_to(row[...], (128, 128)).T

    r, c = iota((432, 162), 0), iota((432, 162), 1)
    first, place = lax.shift_right_logical(r, 4) * 6, r & 15
    selx = ones_where((c == first + place) & (place < 6))
    selv = ones_where((c == first + place - 8) & (place >= 8) & (place < 14))
    for k in range(0, n, 768):
        sl = slice(k, k + 768)
        x16[:, sl] = (dot(selx, x_ref[:, sl]) + dot(selv, v_ref[:, sl])).astype(BF)

    def column(k):
        return jnp.concatenate([bias[k]] * (n // 128), 1)

    def group(g):
        return pl.ds(pl.multiple_of(g * 16, 16), 16)

    def both(g):
        h = dot(win2[...], x16[group(g), :])
        act = jnp.tanh(h[:128] + column(0))
        slope = 1.0 - act * act
        tan = slope * h[128:]
        m = dot(wmid2[...], jnp.concatenate([act.astype(BF), tan.astype(BF)], 0))
        act2 = jnp.tanh(m[:128] + column(1))
        grad = column(2) * (1.0 - act2 * act2)
        bk = dot(wback2[...], jnp.concatenate([grad.astype(BF), (act2 * grad * m[128:]).astype(BF)], 0))
        b1 = bk[:128]
        d2 = slope * bk[128:] + act * tan * b1
        oo[group(g), :] = dot(wt2[...], jnp.concatenate([(slope * b1).astype(BF), d2.astype(BF)], 0))

    def value(g):
        act = jnp.tanh(dot(win2[0:128], x16[group(g), :]) + column(0))
        act2 = jnp.tanh(dot(wmid2[0:128, 0:128], act.astype(BF)) + column(1))
        grad = column(2) * (1.0 - act2 * act2)
        b1 = dot(wback2[0:128, 0:128], grad.astype(BF))
        oo[group(g), :] = dot(wt2[:, 0:128], ((1.0 - act * act) * b1).astype(BF))

    def run(body, low, high):
        def step(i, carry):
            for u in range(U):
                body(low + i * U + u)
            return carry
        lax.fori_loop(0, (high - low) // U, step, 0)

    run(both, 0, EARLY)
    if EARLY < 27: run(value, EARLY, 27)

    r, c = iota((162, 432), 0), iota((162, 432), 1)
    first, place = lax.shift_right_logical(c, 4) * 6, c & 15
    pick_s = ones_where((r == first + place) & (place < 6))
    pick_r = ones_where((r == first + place - 8) & (place >= 8) & (place < 14))
    r, c = iota((96, 81), 0), iota((96, 81), 1)
    lane = r & 31
    grad_op = dot_nt(ones_where((c == lax.shift_right_logical(r, 5) * 27 + lane) & (lane < 27)), grad_ref[...]).astype(BF)
    parts = []
    for k in range(0, n, 768):
        sl = slice(k, k + 768)
        stress = dot(pick_s, oo[:, sl].astype(BF)).astype(BF)
        s_ref[:, sl] = stress
        parts.append(dot(grad_op, stress).astype(BF).astype(F32))
    s_copy = pltpu.make_async_copy(s_ref, s_out, s_sem)
    s_copy.start()
    force = jnp.concatenate(parts, 1)
    place = pm_ref[1:2, :]
    high = pm_ref[0:1, :] * 8 + lax.shift_right_logical(place, 2)
    low = place & 3
    masked = jnp.concatenate(
        [jnp.where(low == l, force[a * 32:(a + 1) * 32], 0.0).astype(BF) for a in range(3) for l in range(4)], 0)
    for k in range(2):
        onehot = ones_where(iota((512, n), 0) + k * 512 == high)
        out = dot_nt(onehot, masked).astype(BF)
        for a in range(3):
            send[k * 64:(k + 1) * 64, a] = out[:, a * 128:(a + 1) * 128].reshape(64, 8, 128)

    if REMOTE:
        pl.semaphore_wait(barrier, devices - 1)
        own = pltpu.make_async_copy(send.at[me], recv_ref.at[me], own_sem)
        own.start()

        def push(k, carry):
            t = lax.rem(me + k, devices)
            pltpu.make_async_remote_copy(
                src_ref=send.at[t], dst_ref=recv_ref.at[me], send_sem=send_sem, recv_sem=recv_sem,
                device_id=(lax.div(t, nd), lax.rem(t, nd)), device_id_type=MESH).start()
            return carry

        lax.fori_loop(1, devices, push, 0)

    run(both, EARLY, 27)
    for k in range(0, n, 768):
        sl = slice(k, k + 768)
        r_ref[:, sl] = dot(pick_r, oo[:, sl].astype(BF)).astype(BF)
    r_copy = pltpu.make_async_copy(r_ref, r_out, r_sem)
    r_copy.start()

    node = jnp.floor((conn_ref[0:1, :].astype(F32) + 0.5) * (1.0 / 3.0))
    along = jnp.floor((node + 0.5) * (1.0 / 513.0))
    across = (node - along * 513.0) * 0.5
    half = jnp.where(across >= 128.0, 1.0, 0.0)
    tile, lane = (along + half).astype(jnp.int32), (across - 128.0 * half).astype(jnp.int32)
    density = dens_ref[...].reshape(1, n)
    d1 = density.astype(BF).astype(F32)
    d2 = (density - d1).astype(BF).astype(F32)
    rows = jnp.concatenate(
        [bm_ref[0:1, :].astype(F32), bm_ref[1:2, :].astype(F32), d1, d2, density - d1 - d2, jnp.zeros((3, n), F32)], 0)
    tiles = n // 128
    spread = jnp.concatenate([jnp.where(tile == t, rows, 0.0) for t in range(tiles)], 0).astype(BF)
    sums = dot_nt(spread, ones_where(iota((128, n), 0) == lane))
    sorted_rows = jnp.concatenate([sums[t * 8:(t + 1) * 8] for t in range(tiles)], 1)
    place = sorted_rows[1:2]
    place_high = jnp.floor(place * 0.25)
    slot = (sorted_rows[0:1] * 8.0 + place_high).astype(jnp.int32)
    low = (place - 4.0 * place_high).astype(jnp.int32)
    for k in range(0, n, 768):
        sl = slice(k, k + 768)
        pick[:, sl] = ones_where(iota((1024, 768), 0) == slot[:, sl])

    own.wait()
    every = pltpu.make_async_remote_copy(
        src_ref=send.at[pl.ds(0, devices - 1)], dst_ref=recv_ref.at[pl.ds(0, devices - 1)],
        send_sem=send_sem, recv_sem=recv_sem, device_id=(b, d), device_id_type=MESH)
    every.wait_send()
    every.wait_recv()

    slots = jnp.concatenate([recv_ref[:, a].reshape(1024, 128) for a in range(3)], 1)
    line = iota((32, 768), 0)

    def take(k):
        sl = slice(k, k + 768)
        found = lax.dot_general(slots, pick[:, sl], (((0,), (0,)), ((), ())), preferred_element_type=F32)
        for a in range(3):
            total = jnp.where(line == 27, sorted_rows[2 + a:3 + a, sl], 0.0)
            for l in range(4):
                total = total + jnp.where(low[:, sl] == l, found[a * 128 + l * 32:a * 128 + (l + 1) * 32], 0.0)
            grid_ref[a * 32:(a + 1) * 32, sl] = total.astype(BF)

    to_right = pltpu.make_async_remote_copy(
        src_ref=grid_ref.at[:, pl.ds(n - 768, 768)], dst_ref=left_ref, send_sem=right_send, recv_sem=left_recv,
        device_id=(b, lax.rem(d + 1, nd)), device_id_type=MESH)
    to_left = pltpu.make_async_remote_copy(
        src_ref=grid_ref.at[:, pl.ds(0, 768)], dst_ref=right_ref, send_sem=left_send, recv_sem=right_recv,
        device_id=(b, lax.rem(d + nd - 1, nd)), device_id_type=MESH)
    not_first, not_last = d > 0, d < nd - 1
    take(0)
    pl.when(not_first)(to_left.start)
    take(n - 768)
    pl.when(not_last)(to_right.start)
    for k in range(768, n - 768, 768):
        take(k)
    s_copy.wait()
    r_copy.wait()

    @pl.when(not_first)
    def _():
        to_left.wait_send()
        to_right.wait_recv()

    @pl.when(not_last)
    def _():
        to_right.wait_send()
        to_left.wait_recv()

    @pl.when(d == 0)
    def _():
        left_ref[...] = jnp.zeros((96, 768), BF)

    @pl.when(d == nd - 1)
    def _():
        right_ref[...] = jnp.zeros((96, 768), BF)


def pointwise(strain, rate, part_map, brick_map, connectivity, density, weight_in, bias_in, weight_mid, bias_mid, weight_out,
              grad_operator):
    n = strain.shape[1]
    row = lambda a: a.reshape(1, 128)
    points = jax.ShapeDtypeStruct((162, n), BF)
    halo = jax.ShapeDtypeStruct((96, 768), BF)
    vmem = pl.BlockSpec(memory_space=pltpu.VMEM)
    anywhere = pl.BlockSpec(memory_space=pl.ANY)
    return pl.pallas_call(
        pointwise_kernel,
        out_shape=(points, points, jax.ShapeDtypeStruct((96, n), BF), halo, halo),
        in_specs=[vmem] * 12,
        out_specs=(anywhere,) * 2 + (vmem,) * 3,
        scratch_shapes=[
            pltpu.VMEM((162, n), BF), pltpu.VMEM((162, n), BF),
            pltpu.VMEM((432, n), BF), pltpu.VMEM((432, n), F32), pltpu.VMEM((3, 128, 128), F32), pltpu.VMEM((256, 16), BF),
            pltpu.VMEM((256, 256), BF), pltpu.VMEM((256, 256), BF), pltpu.VMEM((16, 256), BF), pltpu.VMEM((128, 3, 8, 128), BF),
            pltpu.VMEM((128, 3, 8, 128), BF), pltpu.VMEM((1024, n), BF),
        ] + [pltpu.SemaphoreType.DMA] * 9,
        compiler_params=pltpu.CompilerParams(vmem_limit_bytes=60 << 20, collective_id=0, has_side_effects=True),
        name="pointwise",
    )(strain, rate, part_map, brick_map, connectivity, density, weight_in.T, row(bias_in), weight_mid, row(bias_mid), row(weight_out),
      grad_operator.T)

def fe_consts():
    m=np.array([[2,1,0],[1,4,1],[0,1,2]],np.float64)
    def rowof(u,w,z,d): return (u*3+w)*16+z*3+d
    A=np.zeros((144,144)); S=np.zeros((144,96)); dg=np.ones((144,1)); Q=np.zeros((216,144))
    for u in range(3):
     for w in range(3):
      for z in range(3):
       for d in range(3):
        r=rowof(u,w,z,d)
        S[r,d*32+(u*3+w)*3+z]=1
        dg[r]=m[u,u]*m[w,w]*m[z,z]
        Q[((u*3+w)*3+z)*8+d,r]=1
        for u2 in range(3):
         for w2 in range(3):
          for z2 in range(3):
            A[r,rowof(u2,w2,z2,d)]=m[u,u2]*m[w,w2]*m[z,z2]
    nn=np.arange(768); j=nn//3; z=nn%3; src=((j%2)*3+z)*128+j//2
    return A,S,np.tile(dg,(1,128)),Q,src[None,:].astype(np.int32)

def kernelE(s_in,r_in,L,O,Rt,A,S,dg,Q,src,s_out,r_out,out_ref,s_sem,r_sem):
    s_copy=pltpu.make_async_copy(s_in,s_out,s_sem); r_copy=pltpu.make_async_copy(r_in,r_out,r_sem)
    s_copy.start(); r_copy.start()
    ext=jnp.concatenate([L[...],O[...],Rt[...]],1)
    dens=(ext[27:28].astype(F32)+ext[59:60].astype(F32)+ext[91:92].astype(F32))*(1.0/216.0)
    def shl(x):
        n=x.shape[1]; y=pltpu.roll(x,n-1,1)
        i=lax.broadcasted_iota(jnp.int32,(1,n),1)&255
        return jnp.where(i==255,0.0,y)
    def shr(x):
        n=x.shape[1]; y=pltpu.roll(x,1,1)
        i=lax.broadcasted_iota(jnp.int32,(1,n),1)&255
        return jnp.where(i==0,0.0,y)
    def assemble(h):
        g=[h[16*q:16*q+16] for q in range(9)]
        for u in range(3):
            a0,a2=g[u*3],g[u*3+2]
            g[u*3]=a0+shr(a2); g[u*3+2]=a2+shl(a0)
        z=jnp.zeros((16,256),F32); n=h.shape[1]
        for w in range(3):
            b0,b2=g[w],g[6+w]
            g[w]=b0+jnp.concatenate([z,b2[:,:n-256]],1)
            g[6+w]=b2+jnp.concatenate([b0[:,256:],z],1)
        return jnp.concatenate(g,0)
    load=assemble(dot(S[...],ext))
    diag=assemble(dg[:,0:1]*dens)
    hinv=0.5/jnp.where(diag>0.0,diag,1.0)
    c=lambda x: x[:,256:x.shape[1]-256]
    load=c(load); hinv=c(hinv); dens=c(dens)
    f=load*hinv
    for it in range(2):
        fh=f.astype(BF); fl=(f-fh.astype(F32)).astype(BF)
        h=(dot(A[...],fh)+dot(A[...],fl))*dens
        s=assemble(h)
        f=c(f+(load-s)*hinv)
        load=c(load); hinv=c(hinv); dens=c(dens)
    fh=f.astype(BF); fl=(f-fh.astype(F32)).astype(BF)
    parts=[dot(Q[...],fh),dot(Q[...],fl)]
    P=jnp.where(lax.broadcasted_iota(jnp.int32,(768,768),0)==src[...],1.0,0.0).astype(BF)
    lhs=[]
    for half in range(2):
        for p in parts:
            rows=[]
            for i in range(19):
                u,ex=(i%2,i//2) if i<18 else (2,8)
                b=ex*256+half*128
                rows.append(jnp.concatenate([p[((u*3+w)*3+z)*8:((u*3+w)*3+z)*8+8,b:b+128] for w in range(2) for z in range(3)],1))
            lhs.append(jnp.concatenate(rows,0))
    Y=dot(jnp.concatenate(lhs,0).astype(BF),P)
    fs=parts[0]+parts[1]
    for i in range(19):
        u,ex=(i%2,i//2) if i<18 else (2,8)
        r=slice(8*i,8*i+8)
        h0=Y[0:152][r]+Y[152:304][r]; h1=Y[304:456][r]+Y[456:608][r]
        last=[fs[((u*3+2)*3+z)*8:((u*3+2)*3+z)*8+8,ex*256+255:ex*256+256] for z in range(3)]
        val=jnp.concatenate([h0,h1]+last,1)
        out_ref[:,i*1539:(i+1)*1539]=val[0:3]
    s_copy.wait(); r_copy.wait()

def callE(s,r,L,O,Rt):
    A,S,dg,Q,src=fe_consts()
    ops=[s,r,L,O,Rt,jnp.asarray(A,BF),jnp.asarray(S,BF),jnp.asarray(dg,F32),jnp.asarray(Q,BF),jnp.asarray(src)]
    vmem=pl.BlockSpec(memory_space=pltpu.VMEM); anywhere=pl.BlockSpec(memory_space=pl.ANY)
    point=jax.ShapeDtypeStruct(s.shape,BF)
    return pl.pallas_call(kernelE,out_shape=(point,point,jax.ShapeDtypeStruct((3,29241),F32)),
      in_specs=[anywhere]*2+[vmem]*(len(ops)-2),out_specs=(anywhere,anywhere,vmem),
      scratch_shapes=[pltpu.SemaphoreType.DMA]*2,
      compiler_params=pltpu.CompilerParams(vmem_limit_bytes=60<<20),name="project")(*ops)


def per_device(*arguments):
    stress, stress_rate, grid, left, right = pointwise(*arguments)
    return callE(stress, stress_rate, left, grid, right)


def solution(mesh):
    split = P(None, ("brick", "dom"))
    return jax.shard_map(
        per_device,
        mesh=mesh,
        in_specs=(split,) * 5 + (P(("brick", "dom")),) + (P(),) * 6,
        out_specs=(split,) * 3,
        check_vma=False,
    )
```

```python
import functools

import jax
import jax.numpy as jnp
import numpy as np
from jax import lax
from jax.experimental import pallas as pl
from jax.experimental.pallas import tpu as pltpu
from jax.sharding import PartitionSpec as P

BF=jnp.bfloat16; F32=jnp.float32
def dot(a,b): return jnp.dot(a,b,preferred_element_type=F32)
def dot_nt(a,b): return lax.dot_general(a,b,(((1,),(1,)),((),())),preferred_element_type=F32)
MESH=pl.DeviceIdType.MESH
EARLY=17
U=1
REMOTE=True


def iota(shape, axis):
    return lax.broadcasted_iota(jnp.int32, shape, axis)


def ones_where(mask):
    return jnp.where(mask, 1.0, 0.0).astype(BF)


def pointwise_kernel(x_ref, v_ref, pm_ref, bm_ref, conn_ref, dens_ref, win_ref, bin_ref, wmid_ref, bmid_ref, wout_ref, grad_ref,
                     s_out, r_out, grid_ref, left_ref, right_ref, s_ref, r_ref, x16, oo, bias, win2, wmid2, wback2, wt2, send,
                     recv_ref, pick, send_sem, recv_sem, own_sem, s_sem, r_sem, left_send, left_recv, right_send, right_recv):
    n = x_ref.shape[1]
    if REMOTE:
        nb, nd = lax.axis_size("brick"), lax.axis_size("dom")
        devices = nb * nd
        b, d = lax.axis_index("brick"), lax.axis_index("dom")
        me = b * nd + d
        barrier = pltpu.get_barrier_semaphore()

        def greet(k, carry):
            t = lax.rem(me + k, devices)
            pl.semaphore_signal(barrier, inc=1, device_id=(lax.div(t, nd), lax.rem(t, nd)), device_id_type=MESH)
            return carry

        lax.fori_loop(1, devices, greet, 0)

    win = win_ref[...].astype(F32).T.astype(BF)
    e16 = lambda k: ones_where(iota((6, 16), 1) == iota((6, 16), 0) + k)
    win2[0:128] = dot(win, e16(0)).astype(BF)
    win2[128:256] = dot(win, e16(8)).astype(BF)
    wmid = wmid_ref[...]
    zero = jnp.zeros((128, 128), BF)
    wmid2[...] = jnp.concatenate([jnp.concatenate([wmid, zero], 1), jnp.concatenate([zero, wmid], 1)], 0)
    back = wmid.astype(F32).T.astype(BF)
    wback2[...] = jnp.concatenate([jnp.concatenate([back, zero], 1), jnp.concatenate([zero, back], 1)], 0)
    e = lambda k: ones_where(iota((16, 6), 0) == iota((16, 6), 1) + k)
    wt2[...] = jnp.concatenate([dot_nt(e(0), win).astype(BF), (-2.0 * dot_nt(e(8), win)).astype(BF)], 1)
    for k, row in enumerate((bin_ref, bmid_ref, wout_ref)):
        bias[k] = jnp.broadcast_to(row[...], (128, 128)).T

    r, c = iota((432, 162), 0), iota((432, 162), 1)
    first, place = lax.shift_right_logical(r, 4) * 6, r & 15
    selx = ones_where((c == first + place) & (place < 6))
    selv = ones_where((c == first + place - 8) & (place >= 8) & (place < 14))
    for k in range(0, n, 768):
        sl = slice(k, k + 768)
        x16[:, sl] = (dot(selx, x_ref[:, sl]) + dot(selv, v_ref[:, sl])).astype(BF)

    def column(k):
        return jnp.concatenate([bias[k]] * (n // 128), 1)

    def group(g):
        return pl.ds(pl.multiple_of(g * 16, 16), 16)

    def both(g):
        h = dot(win2[...], x16[group(g), :])
        act = jnp.tanh(h[:128] + column(0))
        slope = 1.0 - act * act
        tan = slope * h[128:]
        m = dot(wmid2[...], jnp.concatenate([act.astype(BF), tan.astype(BF)], 0))
        act2 = jnp.tanh(m[:128] + column(1))
        grad = column(2) * (1.0 - act2 * act2)
        bk = dot(wback2[...], jnp.concatenate([grad.astype(BF), (act2 * grad * m[128:]).astype(BF)], 0))
        b1 = bk[:128]
        d2 = slope * bk[128:] + act * tan * b1
        oo[group(g), :] = dot(wt2[...], jnp.concatenate([(slope * b1).astype(BF), d2.astype(BF)], 0))

    def value(g):
        act = jnp.tanh(dot(win2[0:128], x16[group(g), :]) + column(0))
        act2 = jnp.tanh(dot(wmid2[0:128, 0:128], act.astype(BF)) + column(1))
        grad = column(2) * (1.0 - act2 * act2)
        b1 = dot(wback2[0:128, 0:128], grad.astype(BF))
        oo[group(g), :] = dot(wt2[:, 0:128], ((1.0 - act * act) * b1).astype(BF))

    def run(body, low, high):
        def step(i, carry):
            for u in range(U):
                body(low + i * U + u)
            return carry
        lax.fori_loop(0, (high - low) // U, step, 0)

    run(both, 0, EARLY)
    if EARLY < 27: run(value, EARLY, 27)

    r, c = iota((162, 432), 0), iota((162, 432), 1)
    first, place = lax.shift_right_logical(c, 4) * 6, c & 15
    pick_s = ones_where((r == first + place) & (place < 6))
    pick_r = ones_where((r == first + place - 8) & (place >= 8) & (place < 14))
    r, c = iota((96, 81), 0), iota((96, 81), 1)
    lane = r & 31
    grad_op = dot_nt(ones_where((c == lax.shift_right_logical(r, 5) * 27 + lane) & (lane < 27)), grad_ref[...]).astype(BF)
    parts = []
    for k in range(0, n, 768):
        sl = slice(k, k + 768)
        stress = dot(pick_s, oo[:, sl].astype(BF)).astype(BF)
        s_ref[:, sl] = stress
        parts.append(dot(grad_op, stress).astype(BF).astype(F32))
    s_copy = pltpu.make_async_copy(s_ref, s_out, s_sem)
    s_copy.start()
    force = jnp.concatenate(parts, 1)
    place = pm_ref[1:2, :]
    high = pm_ref[0:1, :] * 8 + lax.shift_right_logical(place, 2)
    low = place & 3
    masked = jnp.concatenate(
        [jnp.where(low == l, force[a * 32:(a + 1) * 32], 0.0).astype(BF) for a in range(3) for l in range(4)], 0)
    for k in range(2):
        onehot = ones_where(iota((512, n), 0) + k * 512 == high)
        out = dot_nt(onehot, masked).astype(BF)
        for a in range(3):
            send[k * 64:(k + 1) * 64, a] = out[:, a * 128:(a + 1) * 128].reshape(64, 8, 128)

    if REMOTE:
        pl.semaphore_wait(barrier, devices - 1)
        own = pltpu.make_async_copy(send.at[me], recv_ref.at[me], own_sem)
        own.start()

        def push(k, carry):
            t = lax.rem(me + k, devices)
            pltpu.make_async_remote_copy(
                src_ref=send.at[t], dst_ref=recv_ref.at[me], send_sem=send_sem, recv_sem=recv_sem,
                device_id=(lax.div(t, nd), lax.rem(t, nd)), device_id_type=MESH).start()
            return carry

        lax.fori_loop(1, devices, push, 0)

    run(both, EARLY, 27)
    for k in range(0, n, 768):
        sl = slice(k, k + 768)
        r_ref[:, sl] = dot(pick_r, oo[:, sl].astype(BF)).astype(BF)
    r_copy = pltpu.make_async_copy(r_ref, r_out, r_sem)
    r_copy.start()

    node = jnp.floor((conn_ref[0:1, :].astype(F32) + 0.5) * (1.0 / 3.0))
    along = jnp.floor((node + 0.5) * (1.0 / 513.0))
    across = (node - along * 513.0) * 0.5
    half = jnp.where(across >= 128.0, 1.0, 0.0)
    tile, lane = (along + half).astype(jnp.int32), (across - 128.0 * half).astype(jnp.int32)
    density = dens_ref[...].reshape(1, n)
    d1 = density.astype(BF).astype(F32)
    d2 = (density - d1).astype(BF).astype(F32)
    rows = jnp.concatenate(
        [bm_ref[0:1, :].astype(F32), bm_ref[1:2, :].astype(F32), d1, d2, density - d1 - d2, jnp.zeros((3, n), F32)], 0)
    tiles = n // 128
    spread = jnp.concatenate([jnp.where(tile == t, rows, 0.0) for t in range(tiles)], 0).astype(BF)
    sums = dot_nt(spread, ones_where(iota((128, n), 0) == lane))
    sorted_rows = jnp.concatenate([sums[t * 8:(t + 1) * 8] for t in range(tiles)], 1)
    place = sorted_rows[1:2]
    place_high = jnp.floor(place * 0.25)
    slot = (sorted_rows[0:1] * 8.0 + place_high).astype(jnp.int32)
    low = (place - 4.0 * place_high).astype(jnp.int32)
    for k in range(0, n, 768):
        sl = slice(k, k + 768)
        pick[:, sl] = ones_where(iota((1024, 768), 0) == slot[:, sl])

    own.wait()
    every = pltpu.make_async_remote_copy(
        src_ref=send.at[pl.ds(0, devices - 1)], dst_ref=recv_ref.at[pl.ds(0, devices - 1)],
        send_sem=send_sem, recv_sem=recv_sem, device_id=(b, d), device_id_type=MESH)
    every.wait_send()
    every.wait_recv()

    slots = jnp.concatenate([recv_ref[:, a].reshape(1024, 128) for a in range(3)], 1)
    line = iota((32, 768), 0)

    def take(k):
        sl = slice(k, k + 768)
        found = lax.dot_general(slots, pick[:, sl], (((0,), (0,)), ((), ())), preferred_element_type=F32)
        for a in range(3):
            total = jnp.where(line == 27, sorted_rows[2 + a:3 + a, sl], 0.0)
            for l in range(4):
                total = total + jnp.where(low[:, sl] == l, found[a * 128 + l * 32:a * 128 + (l + 1) * 32], 0.0)
            grid_ref[a * 32:(a + 1) * 32, sl] = total.astype(BF)

    to_right = pltpu.make_async_remote_copy(
        src_ref=grid_ref.at[:, pl.ds(n - 768, 768)], dst_ref=left_ref, send_sem=right_send, recv_sem=left_recv,
        device_id=(b, lax.rem(d + 1, nd)), device_id_type=MESH)
    to_left = pltpu.make_async_remote_copy(
        src_ref=grid_ref.at[:, pl.ds(0, 768)], dst_ref=right_ref, send_sem=left_send, recv_sem=right_recv,
        device_id=(b, lax.rem(d + nd - 1, nd)), device_id_type=MESH)
    not_first, not_last = d > 0, d < nd - 1
    take(0)
    pl.when(not_first)(to_left.start)
    take(n - 768)
    pl.when(not_last)(to_right.start)
    for k in range(768, n - 768, 768):
        take(k)
    s_copy.wait()
    r_copy.wait()

    @pl.when(not_first)
    def _():
        to_left.wait_send()
        to_right.wait_recv()

    @pl.when(not_last)
    def _():
        to_right.wait_send()
        to_left.wait_recv()

    @pl.when(d == 0)
    def _():
        left_ref[...] = jnp.zeros((96, 768), BF)

    @pl.when(d == nd - 1)
    def _():
        right_ref[...] = jnp.zeros((96, 768), BF)


def pointwise(strain, rate, part_map, brick_map, connectivity, density, weight_in, bias_in, weight_mid, bias_mid, weight_out,
              grad_operator):
    n = strain.shape[1]
    row = lambda a: a.reshape(1, 128)
    points = jax.ShapeDtypeStruct((162, n), BF)
    halo = jax.ShapeDtypeStruct((96, 768), BF)
    vmem = pl.BlockSpec(memory_space=pltpu.VMEM)
    anywhere = pl.BlockSpec(memory_space=pl.ANY)
    return pl.pallas_call(
        pointwise_kernel,
        out_shape=(points, points, jax.ShapeDtypeStruct((96, n), BF), halo, halo),
        in_specs=[vmem] * 12,
        out_specs=(anywhere,) * 2 + (vmem,) * 3,
        scratch_shapes=[
            pltpu.VMEM((162, n), BF), pltpu.VMEM((162, n), BF),
            pltpu.VMEM((432, n), BF), pltpu.VMEM((432, n), F32), pltpu.VMEM((3, 128, 128), F32), pltpu.VMEM((256, 16), BF),
            pltpu.VMEM((256, 256), BF), pltpu.VMEM((256, 256), BF), pltpu.VMEM((16, 256), BF), pltpu.VMEM((128, 3, 8, 128), BF),
            pltpu.VMEM((128, 3, 8, 128), BF), pltpu.VMEM((1024, n), BF),
        ] + [pltpu.SemaphoreType.DMA] * 9,
        compiler_params=pltpu.CompilerParams(vmem_limit_bytes=60 << 20, collective_id=0, has_side_effects=True),
        name="pointwise",
    )(strain, rate, part_map, brick_map, connectivity, density, weight_in.T, row(bias_in), weight_mid, row(bias_mid), row(weight_out),
      grad_operator.T)

def fe_consts():
    m=np.array([[2,1,0],[1,4,1],[0,1,2]],np.float64)
    def rowof(u,w,z,d): return (u*3+w)*16+z*3+d
    A=np.zeros((144,144)); S=np.zeros((144,96)); dg=np.ones((144,1)); Q=np.zeros((216,144))
    for u in range(3):
     for w in range(3):
      for z in range(3):
       for d in range(3):
        r=rowof(u,w,z,d)
        S[r,d*32+(u*3+w)*3+z]=1
        dg[r]=m[u,u]*m[w,w]*m[z,z]
        Q[((u*3+w)*3+z)*8+d,r]=1
        for u2 in range(3):
         for w2 in range(3):
          for z2 in range(3):
            A[r,rowof(u2,w2,z2,d)]=m[u,u2]*m[w,w2]*m[z,z2]
    nn=np.arange(768); j=nn//3; z=nn%3; src=((j%2)*3+z)*128+j//2
    return A,S,np.tile(dg,(1,128)),Q,src[None,:].astype(np.int32)

def kernelE(s_in,r_in,L,O,Rt,A,S,dg,Q,src,s_out,r_out,out_ref,s_hold,r_hold,s_sem,r_sem):
    load_s=pltpu.make_async_copy(s_in,s_hold,s_sem); load_r=pltpu.make_async_copy(r_in,r_hold,r_sem)
    load_s.start(); load_r.start()
    s_copy=pltpu.make_async_copy(s_hold,s_out,s_sem); r_copy=pltpu.make_async_copy(r_hold,r_out,r_sem)
    ext=jnp.concatenate([L[...],O[...],Rt[...]],1)
    dens=(ext[27:28].astype(F32)+ext[59:60].astype(F32)+ext[91:92].astype(F32))*(1.0/216.0)
    def shl(x):
        n=x.shape[1]; y=pltpu.roll(x,n-1,1)
        i=lax.broadcasted_iota(jnp.int32,(1,n),1)&255
        return jnp.where(i==255,0.0,y)
    def shr(x):
        n=x.shape[1]; y=pltpu.roll(x,1,1)
        i=lax.broadcasted_iota(jnp.int32,(1,n),1)&255
        return jnp.where(i==0,0.0,y)
    def assemble(h):
        g=[h[16*q:16*q+16] for q in range(9)]
        for u in range(3):
            a0,a2=g[u*3],g[u*3+2]
            g[u*3]=a0+shr(a2); g[u*3+2]=a2+shl(a0)
        z=jnp.zeros((16,256),F32); n=h.shape[1]
        for w in range(3):
            b0,b2=g[w],g[6+w]
            g[w]=b0+jnp.concatenate([z,b2[:,:n-256]],1)
            g[6+w]=b2+jnp.concatenate([b0[:,256:],z],1)
        return jnp.concatenate(g,0)
    load=assemble(dot(S[...],ext))
    diag=assemble(dg[:,0:1]*dens)
    hinv=0.5/jnp.where(diag>0.0,diag,1.0)
    c=lambda x: x[:,256:x.shape[1]-256]
    load=c(load); hinv=c(hinv); dens=c(dens)
    load_s.wait(); load_r.wait()
    s_copy.start(); r_copy.start()
    f=load*hinv
    for it in range(2):
        fh=f.astype(BF); fl=(f-fh.astype(F32)).astype(BF)
        h=(dot(A[...],fh)+dot(A[...],fl))*dens
        s=assemble(h)
        f=c(f+(load-s)*hinv)
        load=c(load); hinv=c(hinv); dens=c(dens)
    fh=f.astype(BF); fl=(f-fh.astype(F32)).astype(BF)
    parts=[dot(Q[...],fh),dot(Q[...],fl)]
    P=jnp.where(lax.broadcasted_iota(jnp.int32,(768,768),0)==src[...],1.0,0.0).astype(BF)
    lhs=[]
    for half in range(2):
        for p in parts:
            rows=[]
            for i in range(19):
                u,ex=(i%2,i//2) if i<18 else (2,8)
                b=ex*256+half*128
                rows.append(jnp.concatenate([p[((u*3+w)*3+z)*8:((u*3+w)*3+z)*8+8,b:b+128] for w in range(2) for z in range(3)],1))
            lhs.append(jnp.concatenate(rows,0))
    Y=dot(jnp.concatenate(lhs,0).astype(BF),P)
    fs=parts[0]+parts[1]
    for i in range(19):
        u,ex=(i%2,i//2) if i<18 else (2,8)
        r=slice(8*i,8*i+8)
        h0=Y[0:152][r]+Y[152:304][r]; h1=Y[304:456][r]+Y[456:608][r]
        last=[fs[((u*3+2)*3+z)*8:((u*3+2)*3+z)*8+8,ex*256+255:ex*256+256] for z in range(3)]
        val=jnp.concatenate([h0,h1]+last,1)
        out_ref[:,i*1539:(i+1)*1539]=val[0:3]
    s_copy.wait(); r_copy.wait()

def callE(s,r,L,O,Rt):
    A,S,dg,Q,src=fe_consts()
    ops=[s,r,L,O,Rt,jnp.asarray(A,BF),jnp.asarray(S,BF),jnp.asarray(dg,F32),jnp.asarray(Q,BF),jnp.asarray(src)]
    vmem=pl.BlockSpec(memory_space=pltpu.VMEM); anywhere=pl.BlockSpec(memory_space=pl.ANY)
    point=jax.ShapeDtypeStruct(s.shape,BF)
    return pl.pallas_call(kernelE,out_shape=(point,point,jax.ShapeDtypeStruct((3,29241),F32)),
      in_specs=[anywhere]*2+[vmem]*(len(ops)-2),out_specs=(anywhere,anywhere,vmem),
      scratch_shapes=[pltpu.VMEM(s.shape,BF)]*2+[pltpu.SemaphoreType.DMA]*2,
      compiler_params=pltpu.CompilerParams(vmem_limit_bytes=60<<20),name="project")(*ops)


def per_device(*arguments):
    stress, stress_rate, grid, left, right = pointwise(*arguments)
    return callE(stress, stress_rate, left, grid, right)


def solution(mesh):
    split = P(None, ("brick", "dom"))
    return jax.shard_map(
        per_device,
        mesh=mesh,
        in_specs=(split,) * 5 + (P(("brick", "dom")),) + (P(),) * 6,
        out_specs=(split,) * 3,
        check_vma=False,
    )
```

```python
import functools

import jax
import jax.numpy as jnp
import numpy as np
from jax import lax
from jax.experimental import pallas as pl
from jax.experimental.pallas import tpu as pltpu
from jax.sharding import PartitionSpec as P

BF=jnp.bfloat16; F32=jnp.float32
def dot(a,b): return jnp.dot(a,b,preferred_element_type=F32)
def dot_nt(a,b): return lax.dot_general(a,b,(((1,),(1,)),((),())),preferred_element_type=F32)
MESH=pl.DeviceIdType.MESH
EARLY=17
KEPT=7
U=1
REMOTE=True


def iota(shape, axis):
    return lax.broadcasted_iota(jnp.int32, shape, axis)


def ones_where(mask):
    return jnp.where(mask, 1.0, 0.0).astype(BF)


def pointwise_kernel(x_ref, v_ref, pm_ref, bm_ref, conn_ref, dens_ref, win_ref, bin_ref, wmid_ref, bmid_ref, wout_ref, grad_ref,
                     s_out, r_out, grid_ref, left_ref, right_ref, s_ref, r_ref, x16, oo, bias, win2, wmid2, wback2, wt2, send,
                     recv_ref, pick, keep, send_sem, recv_sem, own_sem, s_sem, r_sem, left_send, left_recv, right_send, right_recv):
    n = x_ref.shape[1]
    if REMOTE:
        nb, nd = lax.axis_size("brick"), lax.axis_size("dom")
        devices = nb * nd
        b, d = lax.axis_index("brick"), lax.axis_index("dom")
        me = b * nd + d
        barrier = pltpu.get_barrier_semaphore()

        def greet(k, carry):
            t = lax.rem(me + k, devices)
            pl.semaphore_signal(barrier, inc=1, device_id=(lax.div(t, nd), lax.rem(t, nd)), device_id_type=MESH)
            return carry

        lax.fori_loop(1, devices, greet, 0)

    win = win_ref[...].astype(F32).T.astype(BF)
    e16 = lambda k: ones_where(iota((6, 16), 1) == iota((6, 16), 0) + k)
    win2[0:128] = dot(win, e16(0)).astype(BF)
    win2[128:256] = dot(win, e16(8)).astype(BF)
    wmid = wmid_ref[...]
    zero = jnp.zeros((128, 128), BF)
    wmid2[...] = jnp.concatenate([jnp.concatenate([wmid, zero], 1), jnp.concatenate([zero, wmid], 1)], 0)
    back = wmid.astype(F32).T.astype(BF)
    wback2[...] = jnp.concatenate([jnp.concatenate([back, zero], 1), jnp.concatenate([zero, back], 1)], 0)
    e = lambda k: ones_where(iota((16, 6), 0) == iota((16, 6), 1) + k)
    wt2[...] = jnp.concatenate([dot_nt(e(0), win).astype(BF), (-2.0 * dot_nt(e(8), win)).astype(BF)], 1)
    for k, row in enumerate((bin_ref, bmid_ref, wout_ref)):
        bias[k] = jnp.broadcast_to(row[...], (128, 128)).T

    r, c = iota((432, 162), 0), iota((432, 162), 1)
    first, place = lax.shift_right_logical(r, 4) * 6, r & 15
    selx = ones_where((c == first + place) & (place < 6))
    selv = ones_where((c == first + place - 8) & (place >= 8) & (place < 14))
    for k in range(0, n, 768):
        sl = slice(k, k + 768)
        x16[:, sl] = (dot(selx, x_ref[:, sl]) + dot(selv, v_ref[:, sl])).astype(BF)

    def column(k):
        return jnp.concatenate([bias[k]] * (n // 128), 1)

    def group(g):
        return pl.ds(pl.multiple_of(g * 16, 16), 16)

    def both(g):
        h = dot(win2[...], x16[group(g), :])
        act = jnp.tanh(h[:128] + column(0))
        slope = 1.0 - act * act
        tan = slope * h[128:]
        m = dot(wmid2[...], jnp.concatenate([act.astype(BF), tan.astype(BF)], 0))
        act2 = jnp.tanh(m[:128] + column(1))
        grad = column(2) * (1.0 - act2 * act2)
        bk = dot(wback2[...], jnp.concatenate([grad.astype(BF), (act2 * grad * m[128:]).astype(BF)], 0))
        b1 = bk[:128]
        d2 = slope * bk[128:] + act * tan * b1
        oo[group(g), :] = dot(wt2[...], jnp.concatenate([(slope * b1).astype(BF), d2.astype(BF)], 0))

    def value(g):
        act = jnp.tanh(dot(win2[0:128], x16[group(g), :]) + column(0))
        act2 = jnp.tanh(dot(wmid2[0:128, 0:128], act.astype(BF)) + column(1))
        grad = column(2) * (1.0 - act2 * act2)
        b1 = dot(wback2[0:128, 0:128], grad.astype(BF))
        oo[group(g), :] = dot(wt2[:, 0:128], ((1.0 - act * act) * b1).astype(BF))

    def value_keep(g):
        act = jnp.tanh(dot(win2[0:128], x16[group(g), :]) + column(0))
        act2 = jnp.tanh(dot(wmid2[0:128, 0:128], act.astype(BF)) + column(1))
        grad = column(2) * (1.0 - act2 * act2)
        b1 = dot(wback2[0:128, 0:128], grad.astype(BF))
        oo[group(g), :] = dot(wt2[:, 0:128], ((1.0 - act * act) * b1).astype(BF))
        keep[g - EARLY, 0] = act
        keep[g - EARLY, 1] = act2 * grad
        keep[g - EARLY, 2] = b1

    def rate(g):
        act = keep[g - EARLY, 0]
        slope = 1.0 - act * act
        tan = slope * dot(win2[128:256], x16[group(g), :])
        curv = keep[g - EARLY, 1] * dot(wmid2[0:128, 0:128], tan.astype(BF))
        b2 = dot(wback2[0:128, 0:128], curv.astype(BF))
        d2 = slope * b2 + act * tan * keep[g - EARLY, 2]
        oo[pl.ds(pl.multiple_of(g * 16 + 8, 8), 8), :] = dot(wt2[:, 128:256], d2.astype(BF))[8:16]

    def run(body, low, high):
        def step(i, carry):
            for u in range(U):
                body(low + i * U + u)
            return carry
        lax.fori_loop(0, (high - low) // U, step, 0)

    run(both, 0, EARLY)
    run(value_keep, EARLY, EARLY + KEPT)
    run(value, EARLY + KEPT, 27)

    r, c = iota((162, 432), 0), iota((162, 432), 1)
    first, place = lax.shift_right_logical(c, 4) * 6, c & 15
    pick_s = ones_where((r == first + place) & (place < 6))
    pick_r = ones_where((r == first + place - 8) & (place >= 8) & (place < 14))
    r, c = iota((96, 81), 0), iota((96, 81), 1)
    lane = r & 31
    grad_op = dot_nt(ones_where((c == lax.shift_right_logical(r, 5) * 27 + lane) & (lane < 27)), grad_ref[...]).astype(BF)
    parts = []
    for k in range(0, n, 768):
        sl = slice(k, k + 768)
        stress = dot(pick_s, oo[:, sl].astype(BF)).astype(BF)
        s_ref[:, sl] = stress
        parts.append(dot(grad_op, stress).astype(BF).astype(F32))
    s_copy = pltpu.make_async_copy(s_ref, s_out, s_sem)
    s_copy.start()
    force = jnp.concatenate(parts, 1)
    place = pm_ref[1:2, :]
    high = pm_ref[0:1, :] * 8 + lax.shift_right_logical(place, 2)
    low = place & 3
    masked = jnp.concatenate(
        [jnp.where(low == l, force[a * 32:(a + 1) * 32], 0.0).astype(BF) for a in range(3) for l in range(4)], 0)
    for k in range(2):
        onehot = ones_where(iota((512, n), 0) + k * 512 == high)
        out = dot_nt(onehot, masked).astype(BF)
        for a in range(3):
            send[k * 64:(k + 1) * 64, a] = out[:, a * 128:(a + 1) * 128].reshape(64, 8, 128)

    if REMOTE:
        pl.semaphore_wait(barrier, devices - 1)
        own = pltpu.make_async_copy(send.at[me], recv_ref.at[me], own_sem)
        own.start()

        def push(k, carry):
            t = lax.rem(me + k, devices)
            pltpu.make_async_remote_copy(
                src_ref=send.at[t], dst_ref=recv_ref.at[me], send_sem=send_sem, recv_sem=recv_sem,
                device_id=(lax.div(t, nd), lax.rem(t, nd)), device_id_type=MESH).start()
            return carry

        lax.fori_loop(1, devices, push, 0)

    run(rate, EARLY, EARLY + KEPT)
    run(both, EARLY + KEPT, 27)
    for k in range(0, n, 768):
        sl = slice(k, k + 768)
        r_ref[:, sl] = dot(pick_r, oo[:, sl].astype(BF)).astype(BF)
    r_copy = pltpu.make_async_copy(r_ref, r_out, r_sem)
    r_copy.start()

    node = jnp.floor((conn_ref[0:1, :].astype(F32) + 0.5) * (1.0 / 3.0))
    along = jnp.floor((node + 0.5) * (1.0 / 513.0))
    across = (node - along * 513.0) * 0.5
    half = jnp.where(across >= 128.0, 1.0, 0.0)
    tile, lane = (along + half).astype(jnp.int32), (across - 128.0 * half).astype(jnp.int32)
    density = dens_ref[...].reshape(1, n)
    d1 = density.astype(BF).astype(F32)
    d2 = (density - d1).astype(BF).astype(F32)
    rows = jnp.concatenate(
        [bm_ref[0:1, :].astype(F32), bm_ref[1:2, :].astype(F32), d1, d2, density - d1 - d2, jnp.zeros((3, n), F32)], 0)
    tiles = n // 128
    spread = jnp.concatenate([jnp.where(tile == t, rows, 0.0) for t in range(tiles)], 0).astype(BF)
    sums = dot_nt(spread, ones_where(iota((128, n), 0) == lane))
    sorted_rows = jnp.concatenate([sums[t * 8:(t + 1) * 8] for t in range(tiles)], 1)
    place = sorted_rows[1:2]
    place_high = jnp.floor(place * 0.25)
    slot = (sorted_rows[0:1] * 8.0 + place_high).astype(jnp.int32)
    low = (place - 4.0 * place_high).astype(jnp.int32)
    for k in range(0, n, 768):
        sl = slice(k, k + 768)
        pick[:, sl] = ones_where(iota((1024, 768), 0) == slot[:, sl])

    own.wait()
    every = pltpu.make_async_remote_copy(
        src_ref=send.at[pl.ds(0, devices - 1)], dst_ref=recv_ref.at[pl.ds(0, devices - 1)],
        send_sem=send_sem, recv_sem=recv_sem, device_id=(b, d), device_id_type=MESH)
    every.wait_send()
    every.wait_recv()

    slots = jnp.concatenate([recv_ref[:, a].reshape(1024, 128) for a in range(3)], 1)
    line = iota((32, 768), 0)

    def take(k):
        sl = slice(k, k + 768)
        found = lax.dot_general(slots, pick[:, sl], (((0,), (0,)), ((), ())), preferred_element_type=F32)
        for a in range(3):
            total = jnp.where(line == 27, sorted_rows[2 + a:3 + a, sl], 0.0)
            for l in range(4):
                total = total + jnp.where(low[:, sl] == l, found[a * 128 + l * 32:a * 128 + (l + 1) * 32], 0.0)
            grid_ref[a * 32:(a + 1) * 32, sl] = total.astype(BF)

    to_right = pltpu.make_async_remote_copy(
        src_ref=grid_ref.at[:, pl.ds(n - 768, 768)], dst_ref=left_ref, send_sem=right_send, recv_sem=left_recv,
        device_id=(b, lax.rem(d + 1, nd)), device_id_type=MESH)
    to_left = pltpu.make_async_remote_copy(
        src_ref=grid_ref.at[:, pl.ds(0, 768)], dst_ref=right_ref, send_sem=left_send, recv_sem=right_recv,
        device_id=(b, lax.rem(d + nd - 1, nd)), device_id_type=MESH)
    not_first, not_last = d > 0, d < nd - 1
    take(0)
    pl.when(not_first)(to_left.start)
    take(n - 768)
    pl.when(not_last)(to_right.start)
    for k in range(768, n - 768, 768):
        take(k)
    s_copy.wait()
    r_copy.wait()

    @pl.when(not_first)
    def _():
        to_left.wait_send()
        to_right.wait_recv()

    @pl.when(not_last)
    def _():
        to_right.wait_send()
        to_left.wait_recv()

    @pl.when(d == 0)
    def _():
        left_ref[...] = jnp.zeros((96, 768), BF)

    @pl.when(d == nd - 1)
    def _():
        right_ref[...] = jnp.zeros((96, 768), BF)


def pointwise(strain, rate, part_map, brick_map, connectivity, density, weight_in, bias_in, weight_mid, bias_mid, weight_out,
              grad_operator):
    n = strain.shape[1]
    row = lambda a: a.reshape(1, 128)
    points = jax.ShapeDtypeStruct((162, n), BF)
    halo = jax.ShapeDtypeStruct((96, 768), BF)
    vmem = pl.BlockSpec(memory_space=pltpu.VMEM)
    anywhere = pl.BlockSpec(memory_space=pl.ANY)
    return pl.pallas_call(
        pointwise_kernel,
        out_shape=(points, points, jax.ShapeDtypeStruct((96, n), BF), halo, halo),
        in_specs=[vmem] * 12,
        out_specs=(anywhere,) * 2 + (vmem,) * 3,
        scratch_shapes=[
            pltpu.VMEM((162, n), BF), pltpu.VMEM((162, n), BF),
            pltpu.VMEM((432, n), BF), pltpu.VMEM((432, n), F32), pltpu.VMEM((3, 128, 128), F32), pltpu.VMEM((256, 16), BF),
            pltpu.VMEM((256, 256), BF), pltpu.VMEM((256, 256), BF), pltpu.VMEM((16, 256), BF), pltpu.VMEM((128, 3, 8, 128), BF),
            pltpu.VMEM((128, 3, 8, 128), BF), pltpu.VMEM((1024, n), BF), pltpu.VMEM((KEPT, 3, 128, n), F32),
        ] + [pltpu.SemaphoreType.DMA] * 9,
        compiler_params=pltpu.CompilerParams(vmem_limit_bytes=60 << 20, collective_id=0, has_side_effects=True),
        name="pointwise",
    )(strain, rate, part_map, brick_map, connectivity, density, weight_in.T, row(bias_in), weight_mid, row(bias_mid), row(weight_out),
      grad_operator.T)

def fe_consts():
    m=np.array([[2,1,0],[1,4,1],[0,1,2]],np.float64)
    def rowof(u,w,z,d): return (u*3+w)*16+z*3+d
    A=np.zeros((144,144)); S=np.zeros((144,96)); dg=np.ones((144,1)); Q=np.zeros((216,144))
    for u in range(3):
     for w in range(3):
      for z in range(3):
       for d in range(3):
        r=rowof(u,w,z,d)
        S[r,d*32+(u*3+w)*3+z]=1
        dg[r]=m[u,u]*m[w,w]*m[z,z]
        Q[((u*3+w)*3+z)*8+d,r]=1
        for u2 in range(3):
         for w2 in range(3):
          for z2 in range(3):
            A[r,rowof(u2,w2,z2,d)]=m[u,u2]*m[w,w2]*m[z,z2]
    nn=np.arange(768); j=nn//3; z=nn%3; src=((j%2)*3+z)*128+j//2
    return A,S,np.tile(dg,(1,128)),Q,src[None,:].astype(np.int32)

def kernelE(s_in,r_in,L,O,Rt,A,S,dg,Q,src,s_out,r_out,out_ref,s_hold,r_hold,s_sem,r_sem):
    load_s=pltpu.make_async_copy(s_in,s_hold,s_sem); load_r=pltpu.make_async_copy(r_in,r_hold,r_sem)
    load_s.start(); load_r.start()
    s_copy=pltpu.make_async_copy(s_hold,s_out,s_sem); r_copy=pltpu.make_async_copy(r_hold,r_out,r_sem)
    ext=jnp.concatenate([L[...],O[...],Rt[...]],1)
    dens=(ext[27:28].astype(F32)+ext[59:60].astype(F32)+ext[91:92].astype(F32))*(1.0/216.0)
    def shl(x):
        n=x.shape[1]; y=pltpu.roll(x,n-1,1)
        i=lax.broadcasted_iota(jnp.int32,(1,n),1)&255
        return jnp.where(i==255,0.0,y)
    def shr(x):
        n=x.shape[1]; y=pltpu.roll(x,1,1)
        i=lax.broadcasted_iota(jnp.int32,(1,n),1)&255
        return jnp.where(i==0,0.0,y)
    def assemble(h):
        g=[h[16*q:16*q+16] for q in range(9)]
        for u in range(3):
            a0,a2=g[u*3],g[u*3+2]
            g[u*3]=a0+shr(a2); g[u*3+2]=a2+shl(a0)
        z=jnp.zeros((16,256),F32); n=h.shape[1]
        for w in range(3):
            b0,b2=g[w],g[6+w]
            g[w]=b0+jnp.concatenate([z,b2[:,:n-256]],1)
            g[6+w]=b2+jnp.concatenate([b0[:,256:],z],1)
        return jnp.concatenate(g,0)
    load=assemble(dot(S[...],ext))
    diag=assemble(dg[:,0:1]*dens)
    hinv=0.5/jnp.where(diag>0.0,diag,1.0)
    c=lambda x: x[:,256:x.shape[1]-256]
    load=c(load); hinv=c(hinv); dens=c(dens)
    load_s.wait(); load_r.wait()
    s_copy.start(); r_copy.start()
    f=load*hinv
    for it in range(2):
        fh=f.astype(BF); fl=(f-fh.astype(F32)).astype(BF)
        h=(dot(A[...],fh)+dot(A[...],fl))*dens
        s=assemble(h)
        f=c(f+(load-s)*hinv)
        load=c(load); hinv=c(hinv); dens=c(dens)
    fh=f.astype(BF); fl=(f-fh.astype(F32)).astype(BF)
    parts=[dot(Q[...],fh),dot(Q[...],fl)]
    P=jnp.where(lax.broadcasted_iota(jnp.int32,(768,768),0)==src[...],1.0,0.0).astype(BF)
    lhs=[]
    for half in range(2):
        for p in parts:
            rows=[]
            for i in range(19):
                u,ex=(i%2,i//2) if i<18 else (2,8)
                b=ex*256+half*128
                rows.append(jnp.concatenate([p[((u*3+w)*3+z)*8:((u*3+w)*3+z)*8+8,b:b+128] for w in range(2) for z in range(3)],1))
            lhs.append(jnp.concatenate(rows,0))
    Y=dot(jnp.concatenate(lhs,0).astype(BF),P)
    fs=parts[0]+parts[1]
    for i in range(19):
        u,ex=(i%2,i//2) if i<18 else (2,8)
        r=slice(8*i,8*i+8)
        h0=Y[0:152][r]+Y[152:304][r]; h1=Y[304:456][r]+Y[456:608][r]
        last=[fs[((u*3+2)*3+z)*8:((u*3+2)*3+z)*8+8,ex*256+255:ex*256+256] for z in range(3)]
        val=jnp.concatenate([h0,h1]+last,1)
        out_ref[:,i*1539:(i+1)*1539]=val[0:3]
    s_copy.wait(); r_copy.wait()

def callE(s,r,L,O,Rt):
    A,S,dg,Q,src=fe_consts()
    ops=[s,r,L,O,Rt,jnp.asarray(A,BF),jnp.asarray(S,BF),jnp.asarray(dg,F32),jnp.asarray(Q,BF),jnp.asarray(src)]
    vmem=pl.BlockSpec(memory_space=pltpu.VMEM); anywhere=pl.BlockSpec(memory_space=pl.ANY)
    point=jax.ShapeDtypeStruct(s.shape,BF)
    return pl.pallas_call(kernelE,out_shape=(point,point,jax.ShapeDtypeStruct((3,29241),F32)),
      in_specs=[anywhere]*2+[vmem]*(len(ops)-2),out_specs=(anywhere,anywhere,vmem),
      scratch_shapes=[pltpu.VMEM(s.shape,BF)]*2+[pltpu.SemaphoreType.DMA]*2,
      compiler_params=pltpu.CompilerParams(vmem_limit_bytes=60<<20),name="project")(*ops)


def per_device(*arguments):
    stress, stress_rate, grid, left, right = pointwise(*arguments)
    return callE(stress, stress_rate, left, grid, right)


def solution(mesh):
    split = P(None, ("brick", "dom"))
    return jax.shard_map(
        per_device,
        mesh=mesh,
        in_specs=(split,) * 5 + (P(("brick", "dom")),) + (P(),) * 6,
        out_specs=(split,) * 3,
        check_vma=False,
    )
```

```python
import functools

import jax
import jax.numpy as jnp
import numpy as np
from jax import lax
from jax.experimental import pallas as pl
from jax.experimental.pallas import tpu as pltpu
from jax.sharding import PartitionSpec as P

BF=jnp.bfloat16; F32=jnp.float32
def dot(a,b): return jnp.dot(a,b,preferred_element_type=F32)
def dot_nt(a,b): return lax.dot_general(a,b,(((1,),(1,)),((),())),preferred_element_type=F32)
MESH=pl.DeviceIdType.MESH
EARLY=18
KEPT=6
U=3
REMOTE=True


def iota(shape, axis):
    return lax.broadcasted_iota(jnp.int32, shape, axis)


def ones_where(mask):
    return jnp.where(mask, 1.0, 0.0).astype(BF)


def pointwise_kernel(x_ref, v_ref, pm_ref, bm_ref, conn_ref, dens_ref, win_ref, bin_ref, wmid_ref, bmid_ref, wout_ref, grad_ref,
                     s_out, r_out, grid_ref, left_ref, right_ref, s_ref, r_ref, nodes, x16, oo, bias, win2, wmid2, wback2, wt2, send,
                     recv_ref, pick, keep, send_sem, recv_sem, own_sem, s_sem, r_sem, left_send, left_recv, right_send, right_recv,
                     x_sem, v_sem, node_sem):
    n = x_ref.shape[1]
    x_copy = pltpu.make_async_copy(x_ref, s_ref, x_sem)
    v_copy = pltpu.make_async_copy(v_ref, r_ref, v_sem)
    node_copy = pltpu.make_async_copy(conn_ref.at[pl.ds(0, 8)], nodes, node_sem)
    x_copy.start()
    v_copy.start()
    node_copy.start()
    if REMOTE:
        nb, nd = lax.axis_size("brick"), lax.axis_size("dom")
        devices = nb * nd
        b, d = lax.axis_index("brick"), lax.axis_index("dom")
        me = b * nd + d
        barrier = pltpu.get_barrier_semaphore()

        def greet(k, carry):
            t = lax.rem(me + k, devices)
            pl.semaphore_signal(barrier, inc=1, device_id=(lax.div(t, nd), lax.rem(t, nd)), device_id_type=MESH)
            return carry

        lax.fori_loop(1, devices, greet, 0)

    win = win_ref[...].astype(F32).T.astype(BF)
    e16 = lambda k: ones_where(iota((6, 16), 1) == iota((6, 16), 0) + k)
    win2[0:128] = dot(win, e16(0)).astype(BF)
    win2[128:256] = dot(win, e16(8)).astype(BF)
    wmid = wmid_ref[...]
    zero = jnp.zeros((128, 128), BF)
    wmid2[...] = jnp.concatenate([jnp.concatenate([wmid, zero], 1), jnp.concatenate([zero, wmid], 1)], 0)
    back = wmid.astype(F32).T.astype(BF)
    wback2[...] = jnp.concatenate([jnp.concatenate([back, zero], 1), jnp.concatenate([zero, back], 1)], 0)
    e = lambda k: ones_where(iota((16, 6), 0) == iota((16, 6), 1) + k)
    wt2[...] = jnp.concatenate([dot_nt(e(0), win).astype(BF), (-2.0 * dot_nt(e(8), win)).astype(BF)], 1)
    for k, row in enumerate((bin_ref, bmid_ref, wout_ref)):
        bias[k] = jnp.broadcast_to(row[...], (128, 128)).T

    r, c = iota((432, 162), 0), iota((432, 162), 1)
    first, place = lax.shift_right_logical(r, 4) * 6, r & 15
    selx = ones_where((c == first + place) & (place < 6))
    selv = ones_where((c == first + place - 8) & (place >= 8) & (place < 14))
    x_copy.wait()
    v_copy.wait()
    for k in range(0, n, 768):
        sl = slice(k, k + 768)
        x16[:, sl] = (dot(selx, s_ref[:, sl]) + dot(selv, r_ref[:, sl])).astype(BF)

    def column(k):
        return jnp.concatenate([bias[k]] * (n // 128), 1)

    def group(g):
        return pl.ds(pl.multiple_of(g * 16, 16), 16)

    def both(g):
        h = dot(win2[...], x16[group(g), :])
        act = jnp.tanh(h[:128] + column(0))
        slope = 1.0 - act * act
        tan = slope * h[128:]
        m = dot(wmid2[...], jnp.concatenate([act.astype(BF), tan.astype(BF)], 0))
        act2 = jnp.tanh(m[:128] + column(1))
        grad = column(2) * (1.0 - act2 * act2)
        bk = dot(wback2[...], jnp.concatenate([grad.astype(BF), (act2 * grad * m[128:]).astype(BF)], 0))
        b1 = bk[:128]
        d2 = slope * bk[128:] + act * tan * b1
        oo[group(g), :] = dot(wt2[...], jnp.concatenate([(slope * b1).astype(BF), d2.astype(BF)], 0))

    def value(g):
        act = jnp.tanh(dot(win2[0:128], x16[group(g), :]) + column(0))
        act2 = jnp.tanh(dot(wmid2[0:128, 0:128], act.astype(BF)) + column(1))
        grad = column(2) * (1.0 - act2 * act2)
        b1 = dot(wback2[0:128, 0:128], grad.astype(BF))
        oo[group(g), :] = dot(wt2[:, 0:128], ((1.0 - act * act) * b1).astype(BF))

    def value_keep(g):
        act = jnp.tanh(dot(win2[0:128], x16[group(g), :]) + column(0))
        act2 = jnp.tanh(dot(wmid2[0:128, 0:128], act.astype(BF)) + column(1))
        grad = column(2) * (1.0 - act2 * act2)
        b1 = dot(wback2[0:128, 0:128], grad.astype(BF))
        oo[group(g), :] = dot(wt2[:, 0:128], ((1.0 - act * act) * b1).astype(BF))
        keep[g - EARLY, 0] = act
        keep[g - EARLY, 1] = act2 * grad
        keep[g - EARLY, 2] = b1

    def rate(g):
        act = keep[g - EARLY, 0]
        slope = 1.0 - act * act
        tan = slope * dot(win2[128:256], x16[group(g), :])
        curv = keep[g - EARLY, 1] * dot(wmid2[0:128, 0:128], tan.astype(BF))
        b2 = dot(wback2[0:128, 0:128], curv.astype(BF))
        d2 = slope * b2 + act * tan * keep[g - EARLY, 2]
        oo[pl.ds(pl.multiple_of(g * 16 + 8, 8), 8), :] = dot(wt2[:, 128:256], d2.astype(BF))[8:16]

    def run(body, low, high):
        def step(i, carry):
            for u in range(U):
                body(low + i * U + u)
            return carry
        lax.fori_loop(0, (high - low) // U, step, 0)

    run(both, 0, EARLY)
    run(value_keep, EARLY, EARLY + KEPT)
    run(value, EARLY + KEPT, 27)

    r, c = iota((162, 432), 0), iota((162, 432), 1)
    first, place = lax.shift_right_logical(c, 4) * 6, c & 15
    pick_s = ones_where((r == first + place) & (place < 6))
    pick_r = ones_where((r == first + place - 8) & (place >= 8) & (place < 14))
    r, c = iota((96, 81), 0), iota((96, 81), 1)
    lane = r & 31
    grad_op = dot_nt(ones_where((c == lax.shift_right_logical(r, 5) * 27 + lane) & (lane < 27)), grad_ref[...]).astype(BF)
    parts = []
    for k in range(0, n, 768):
        sl = slice(k, k + 768)
        stress = dot(pick_s, oo[:, sl].astype(BF)).astype(BF)
        s_ref[:, sl] = stress
        parts.append(dot(grad_op, stress).astype(BF).astype(F32))
    s_copy = pltpu.make_async_copy(s_ref, s_out, s_sem)
    s_copy.start()
    force = jnp.concatenate(parts, 1)
    place = pm_ref[1:2, :]
    high = pm_ref[0:1, :] * 8 + lax.shift_right_logical(place, 2)
    low = place & 3
    masked = jnp.concatenate(
        [jnp.where(low == l, force[a * 32:(a + 1) * 32], 0.0).astype(BF) for a in range(3) for l in range(4)], 0)
    for k in range(2):
        onehot = ones_where(iota((512, n), 0) + k * 512 == high)
        out = dot_nt(onehot, masked).astype(BF)
        for a in range(3):
            send[k * 64:(k + 1) * 64, a] = out[:, a * 128:(a + 1) * 128].reshape(64, 8, 128)

    if REMOTE:
        pl.semaphore_wait(barrier, devices - 1)
        own = pltpu.make_async_copy(send.at[me], recv_ref.at[me], own_sem)
        own.start()

        def push(k, carry):
            t = lax.rem(me + k, devices)
            pltpu.make_async_remote_copy(
                src_ref=send.at[t], dst_ref=recv_ref.at[me], send_sem=send_sem, recv_sem=recv_sem,
                device_id=(lax.div(t, nd), lax.rem(t, nd)), device_id_type=MESH).start()
            return carry

        lax.fori_loop(1, devices, push, 0)

    run(rate, EARLY, EARLY + KEPT)
    run(both, EARLY + KEPT, 27)
    for k in range(0, n, 768):
        sl = slice(k, k + 768)
        r_ref[:, sl] = dot(pick_r, oo[:, sl].astype(BF)).astype(BF)
    r_copy = pltpu.make_async_copy(r_ref, r_out, r_sem)
    r_copy.start()

    node_copy.wait()
    node = jnp.floor((nodes[0:1, :].astype(F32) + 0.5) * (1.0 / 3.0))
    along = jnp.floor((node + 0.5) * (1.0 / 513.0))
    across = (node - along * 513.0) * 0.5
    half = jnp.where(across >= 128.0, 1.0, 0.0)
    tile, lane = (along + half).astype(jnp.int32), (across - 128.0 * half).astype(jnp.int32)
    density = dens_ref[...].reshape(1, n)
    d1 = density.astype(BF).astype(F32)
    d2 = (density - d1).astype(BF).astype(F32)
    rows = jnp.concatenate(
        [bm_ref[0:1, :].astype(F32), bm_ref[1:2, :].astype(F32), d1, d2, density - d1 - d2, jnp.zeros((3, n), F32)], 0)
    tiles = n // 128
    spread = jnp.concatenate([jnp.where(tile == t, rows, 0.0) for t in range(tiles)], 0).astype(BF)
    sums = dot_nt(spread, ones_where(iota((128, n), 0) == lane))
    sorted_rows = jnp.concatenate([sums[t * 8:(t + 1) * 8] for t in range(tiles)], 1)
    place = sorted_rows[1:2]
    place_high = jnp.floor(place * 0.25)
    slot = (sorted_rows[0:1] * 8.0 + place_high).astype(jnp.int32)
    low = (place - 4.0 * place_high).astype(jnp.int32)
    for k in range(0, n, 768):
        sl = slice(k, k + 768)
        pick[:, sl] = ones_where(iota((1024, 768), 0) == slot[:, sl])

    own.wait()
    every = pltpu.make_async_remote_copy(
        src_ref=send.at[pl.ds(0, devices - 1)], dst_ref=recv_ref.at[pl.ds(0, devices - 1)],
        send_sem=send_sem, recv_sem=recv_sem, device_id=(b, d), device_id_type=MESH)
    every.wait_send()
    every.wait_recv()

    slots = jnp.concatenate([recv_ref[:, a].reshape(1024, 128) for a in range(3)], 1)
    line = iota((32, 768), 0)

    def take(k):
        sl = slice(k, k + 768)
        found = lax.dot_general(slots, pick[:, sl], (((0,), (0,)), ((), ())), preferred_element_type=F32)
        for a in range(3):
            total = jnp.where(line == 27, sorted_rows[2 + a:3 + a, sl], 0.0)
            for l in range(4):
                total = total + jnp.where(low[:, sl] == l, found[a * 128 + l * 32:a * 128 + (l + 1) * 32], 0.0)
            grid_ref[a * 32:(a + 1) * 32, sl] = total.astype(BF)

    to_right = pltpu.make_async_remote_copy(
        src_ref=grid_ref.at[:, pl.ds(n - 768, 768)], dst_ref=left_ref, send_sem=right_send, recv_sem=left_recv,
        device_id=(b, lax.rem(d + 1, nd)), device_id_type=MESH)
    to_left = pltpu.make_async_remote_copy(
        src_ref=grid_ref.at[:, pl.ds(0, 768)], dst_ref=right_ref, send_sem=left_send, recv_sem=right_recv,
        device_id=(b, lax.rem(d + nd - 1, nd)), device_id_type=MESH)
    not_first, not_last = d > 0, d < nd - 1
    take(0)
    pl.when(not_first)(to_left.start)
    take(n - 768)
    pl.when(not_last)(to_right.start)
    for k in range(768, n - 768, 768):
        take(k)
    s_copy.wait()
    r_copy.wait()

    @pl.when(not_first)
    def _():
        to_left.wait_send()
        to_right.wait_recv()

    @pl.when(not_last)
    def _():
        to_right.wait_send()
        to_left.wait_recv()

    @pl.when(d == 0)
    def _():
        left_ref[...] = jnp.zeros((96, 768), BF)

    @pl.when(d == nd - 1)
    def _():
        right_ref[...] = jnp.zeros((96, 768), BF)


def pointwise(strain, rate, part_map, brick_map, connectivity, density, weight_in, bias_in, weight_mid, bias_mid, weight_out,
              grad_operator):
    n = strain.shape[1]
    row = lambda a: a.reshape(1, 128)
    points = jax.ShapeDtypeStruct((162, n), BF)
    halo = jax.ShapeDtypeStruct((96, 768), BF)
    vmem = pl.BlockSpec(memory_space=pltpu.VMEM)
    anywhere = pl.BlockSpec(memory_space=pl.ANY)
    return pl.pallas_call(
        pointwise_kernel,
        out_shape=(points, points, jax.ShapeDtypeStruct((96, n), BF), halo, halo),
        in_specs=[anywhere] * 2 + [vmem] * 2 + [anywhere] + [vmem] * 7,
        out_specs=(anywhere,) * 2 + (vmem,) * 3,
        scratch_shapes=[
            pltpu.VMEM((162, n), BF), pltpu.VMEM((162, n), BF), pltpu.VMEM((8, n), jnp.int32),
            pltpu.VMEM((432, n), BF), pltpu.VMEM((432, n), F32), pltpu.VMEM((3, 128, 128), F32), pltpu.VMEM((256, 16), BF),
            pltpu.VMEM((256, 256), BF), pltpu.VMEM((256, 256), BF), pltpu.VMEM((16, 256), BF), pltpu.VMEM((128, 3, 8, 128), BF),
            pltpu.VMEM((128, 3, 8, 128), BF), pltpu.VMEM((1024, n), BF), pltpu.VMEM((KEPT, 3, 128, n), F32),
        ] + [pltpu.SemaphoreType.DMA] * 12,
        compiler_params=pltpu.CompilerParams(vmem_limit_bytes=60 << 20, collective_id=0, has_side_effects=True),
        name="pointwise",
    )(strain, rate, part_map, brick_map, connectivity, density, weight_in.T, row(bias_in), weight_mid, row(bias_mid), row(weight_out),
      grad_operator.T)

def fe_consts():
    m=np.array([[2,1,0],[1,4,1],[0,1,2]],np.float64)
    def rowof(u,w,z,d): return (u*3+w)*16+z*3+d
    A=np.zeros((144,144)); S=np.zeros((144,96)); dg=np.ones((144,1)); Q=np.zeros((216,144))
    for u in range(3):
     for w in range(3):
      for z in range(3):
       for d in range(3):
        r=rowof(u,w,z,d)
        S[r,d*32+(u*3+w)*3+z]=1
        dg[r]=m[u,u]*m[w,w]*m[z,z]
        Q[((u*3+w)*3+z)*8+d,r]=1
        for u2 in range(3):
         for w2 in range(3):
          for z2 in range(3):
            A[r,rowof(u2,w2,z2,d)]=m[u,u2]*m[w,w2]*m[z,z2]
    nn=np.arange(768); j=nn//3; z=nn%3; src=((j%2)*3+z)*128+j//2
    return A,S,np.tile(dg,(1,128)),Q,src[None,:].astype(np.int32)

def kernelE(s_in,r_in,L,O,Rt,A,S,dg,Q,src,s_out,r_out,out_ref,s_hold,r_hold,s_sem,r_sem):
    load_s=pltpu.make_async_copy(s_in,s_hold,s_sem); load_r=pltpu.make_async_copy(r_in,r_hold,r_sem)
    load_s.start(); load_r.start()
    s_copy=pltpu.make_async_copy(s_hold,s_out,s_sem); r_copy=pltpu.make_async_copy(r_hold,r_out,r_sem)
    ext=jnp.concatenate([L[...],O[...],Rt[...]],1)
    dens=(ext[27:28].astype(F32)+ext[59:60].astype(F32)+ext[91:92].astype(F32))*(1.0/216.0)
    def shl(x):
        n=x.shape[1]; y=pltpu.roll(x,n-1,1)
        i=lax.broadcasted_iota(jnp.int32,(1,n),1)&255
        return jnp.where(i==255,0.0,y)
    def shr(x):
        n=x.shape[1]; y=pltpu.roll(x,1,1)
        i=lax.broadcasted_iota(jnp.int32,(1,n),1)&255
        return jnp.where(i==0,0.0,y)
    def assemble(h):
        g=[h[16*q:16*q+16] for q in range(9)]
        for u in range(3):
            a0,a2=g[u*3],g[u*3+2]
            g[u*3]=a0+shr(a2); g[u*3+2]=a2+shl(a0)
        z=jnp.zeros((16,256),F32); n=h.shape[1]
        for w in range(3):
            b0,b2=g[w],g[6+w]
            g[w]=b0+jnp.concatenate([z,b2[:,:n-256]],1)
            g[6+w]=b2+jnp.concatenate([b0[:,256:],z],1)
        return jnp.concatenate(g,0)
    load=assemble(dot(S[...],ext))
    diag=assemble(dg[:,0:1]*dens)
    hinv=0.5/jnp.where(diag>0.0,diag,1.0)
    c=lambda x: x[:,256:x.shape[1]-256]
    load=c(load); hinv=c(hinv); dens=c(dens)
    load_s.wait(); load_r.wait()
    s_copy.start(); r_copy.start()
    f=load*hinv
    for it in range(2):
        fh=f.astype(BF); fl=(f-fh.astype(F32)).astype(BF)
        h=(dot(A[...],fh)+dot(A[...],fl))*dens
        s=assemble(h)
        f=c(f+(load-s)*hinv)
        load=c(load); hinv=c(hinv); dens=c(dens)
    fh=f.astype(BF); fl=(f-fh.astype(F32)).astype(BF)
    parts=[dot(Q[...],fh),dot(Q[...],fl)]
    P=jnp.where(lax.broadcasted_iota(jnp.int32,(768,768),0)==src[...],1.0,0.0).astype(BF)
    lhs=[]
    for half in range(2):
        for p in parts:
            rows=[]
            for i in range(19):
                u,ex=(i%2,i//2) if i<18 else (2,8)
                b=ex*256+half*128
                rows.append(jnp.concatenate([p[((u*3+w)*3+z)*8:((u*3+w)*3+z)*8+8,b:b+128] for w in range(2) for z in range(3)],1))
            lhs.append(jnp.concatenate(rows,0))
    Y=dot(jnp.concatenate(lhs,0).astype(BF),P)
    fs=parts[0]+parts[1]
    for i in range(19):
        u,ex=(i%2,i//2) if i<18 else (2,8)
        r=slice(8*i,8*i+8)
        h0=Y[0:152][r]+Y[152:304][r]; h1=Y[304:456][r]+Y[456:608][r]
        last=[fs[((u*3+2)*3+z)*8:((u*3+2)*3+z)*8+8,ex*256+255:ex*256+256] for z in range(3)]
        val=jnp.concatenate([h0,h1]+last,1)
        out_ref[:,i*1539:(i+1)*1539]=val[0:3]
    s_copy.wait(); r_copy.wait()

def callE(s,r,L,O,Rt):
    A,S,dg,Q,src=fe_consts()
    ops=[s,r,L,O,Rt,jnp.asarray(A,BF),jnp.asarray(S,BF),jnp.asarray(dg,F32),jnp.asarray(Q,BF),jnp.asarray(src)]
    vmem=pl.BlockSpec(memory_space=pltpu.VMEM); anywhere=pl.BlockSpec(memory_space=pl.ANY)
    point=jax.ShapeDtypeStruct(s.shape,BF)
    return pl.pallas_call(kernelE,out_shape=(point,point,jax.ShapeDtypeStruct((3,29241),F32)),
      in_specs=[anywhere]*2+[vmem]*(len(ops)-2),out_specs=(anywhere,anywhere,vmem),
      scratch_shapes=[pltpu.VMEM(s.shape,BF)]*2+[pltpu.SemaphoreType.DMA]*2,
      compiler_params=pltpu.CompilerParams(vmem_limit_bytes=60<<20),name="project")(*ops)


def per_device(*arguments):
    stress, stress_rate, grid, left, right = pointwise(*arguments)
    return callE(stress, stress_rate, left, grid, right)


def solution(mesh):
    split = P(None, ("brick", "dom"))
    return jax.shard_map(
        per_device,
        mesh=mesh,
        in_specs=(split,) * 5 + (P(("brick", "dom")),) + (P(),) * 6,
        out_specs=(split,) * 3,
        check_vma=False,
    )
```

```python
import functools

import jax
import jax.numpy as jnp
import numpy as np
from jax import lax
from jax.experimental import pallas as pl
from jax.experimental.pallas import tpu as pltpu
from jax.sharding import PartitionSpec as P

BF=jnp.bfloat16; F32=jnp.float32
def dot(a,b): return jnp.dot(a,b,preferred_element_type=F32)
def dot_nt(a,b): return lax.dot_general(a,b,(((1,),(1,)),((),())),preferred_element_type=F32)
MESH=pl.DeviceIdType.MESH
EARLY=15
KEPT=12
U=3
REMOTE=True


def iota(shape, axis):
    return lax.broadcasted_iota(jnp.int32, shape, axis)


def ones_where(mask):
    return jnp.where(mask, 1.0, 0.0).astype(BF)


def pointwise_kernel(x_ref, v_ref, pm_ref, bm_ref, conn_ref, dens_ref, win_ref, bin_ref, wmid_ref, bmid_ref, wout_ref, grad_ref,
                     s_out, r_out, grid_ref, left_ref, right_ref, s_ref, r_ref, nodes, x16, oo, bias, win2, wmid2, wback2, wt2, send,
                     recv_ref, pick, kept_act, kept, send_sem, recv_sem, own_sem, s_sem, r_sem, left_send, left_recv, right_send, right_recv,
                     x_sem, v_sem, node_sem):
    n = x_ref.shape[1]
    x_copy = pltpu.make_async_copy(x_ref, s_ref, x_sem)
    v_copy = pltpu.make_async_copy(v_ref, r_ref, v_sem)
    node_copy = pltpu.make_async_copy(conn_ref.at[pl.ds(0, 8)], nodes, node_sem)
    x_copy.start()
    v_copy.start()
    node_copy.start()
    if REMOTE:
        nb, nd = lax.axis_size("brick"), lax.axis_size("dom")
        devices = nb * nd
        b, d = lax.axis_index("brick"), lax.axis_index("dom")
        me = b * nd + d
        barrier = pltpu.get_barrier_semaphore()

        def greet(k, carry):
            t = lax.rem(me + k, devices)
            pl.semaphore_signal(barrier, inc=1, device_id=(lax.div(t, nd), lax.rem(t, nd)), device_id_type=MESH)
            return carry

        lax.fori_loop(1, devices, greet, 0)

    win = win_ref[...].astype(F32).T.astype(BF)
    e16 = lambda k: ones_where(iota((6, 16), 1) == iota((6, 16), 0) + k)
    win2[0:128] = dot(win, e16(0)).astype(BF)
    win2[128:256] = dot(win, e16(8)).astype(BF)
    wmid = wmid_ref[...]
    zero = jnp.zeros((128, 128), BF)
    wmid2[...] = jnp.concatenate([jnp.concatenate([wmid, zero], 1), jnp.concatenate([zero, wmid], 1)], 0)
    back = wmid.astype(F32).T.astype(BF)
    wback2[...] = jnp.concatenate([jnp.concatenate([back, zero], 1), jnp.concatenate([zero, back], 1)], 0)
    e = lambda k: ones_where(iota((16, 6), 0) == iota((16, 6), 1) + k)
    wt2[...] = jnp.concatenate([dot_nt(e(0), win).astype(BF), (-2.0 * dot_nt(e(8), win)).astype(BF)], 1)
    for k, row in enumerate((bin_ref, bmid_ref, wout_ref)):
        bias[k] = jnp.broadcast_to(row[...], (128, 128)).T

    r, c = iota((432, 162), 0), iota((432, 162), 1)
    first, place = lax.shift_right_logical(r, 4) * 6, r & 15
    selx = ones_where((c == first + place) & (place < 6))
    selv = ones_where((c == first + place - 8) & (place >= 8) & (place < 14))
    x_copy.wait()
    v_copy.wait()
    for k in range(0, n, 768):
        sl = slice(k, k + 768)
        x16[:, sl] = (dot(selx, s_ref[:, sl]) + dot(selv, r_ref[:, sl])).astype(BF)

    def column(k):
        return jnp.concatenate([bias[k]] * (n // 128), 1)

    def group(g):
        return pl.ds(pl.multiple_of(g * 16, 16), 16)

    def both(g):
        h = dot(win2[...], x16[group(g), :])
        act = jnp.tanh(h[:128] + column(0))
        slope = 1.0 - act * act
        tan = slope * h[128:]
        m = dot(wmid2[...], jnp.concatenate([act.astype(BF), tan.astype(BF)], 0))
        act2 = jnp.tanh(m[:128] + column(1))
        grad = column(2) * (1.0 - act2 * act2)
        bk = dot(wback2[...], jnp.concatenate([grad.astype(BF), (act2 * grad * m[128:]).astype(BF)], 0))
        b1 = bk[:128]
        d2 = slope * bk[128:] + act * tan * b1
        oo[group(g), :] = dot(wt2[...], jnp.concatenate([(slope * b1).astype(BF), d2.astype(BF)], 0))

    def value(g):
        act = jnp.tanh(dot(win2[0:128], x16[group(g), :]) + column(0))
        act2 = jnp.tanh(dot(wmid2[0:128, 0:128], act.astype(BF)) + column(1))
        grad = column(2) * (1.0 - act2 * act2)
        b1 = dot(wback2[0:128, 0:128], grad.astype(BF))
        oo[group(g), :] = dot(wt2[:, 0:128], ((1.0 - act * act) * b1).astype(BF))

    def value_keep(g):
        act = jnp.tanh(dot(win2[0:128], x16[group(g), :]) + column(0))
        act2 = jnp.tanh(dot(wmid2[0:128, 0:128], act.astype(BF)) + column(1))
        grad = column(2) * (1.0 - act2 * act2)
        b1 = dot(wback2[0:128, 0:128], grad.astype(BF))
        oo[group(g), :] = dot(wt2[:, 0:128], ((1.0 - act * act) * b1).astype(BF))
        kept_act[g - EARLY] = act
        kept[g - EARLY, 0] = (act2 * grad).astype(BF)
        kept[g - EARLY, 1] = b1.astype(BF)

    def rate(g):
        act = kept_act[g - EARLY]
        slope = 1.0 - act * act
        tan = slope * dot(win2[128:256], x16[group(g), :])
        curv = kept[g - EARLY, 0].astype(F32) * dot(wmid2[0:128, 0:128], tan.astype(BF))
        b2 = dot(wback2[0:128, 0:128], curv.astype(BF))
        d2 = slope * b2 + act * tan * kept[g - EARLY, 1].astype(F32)
        oo[pl.ds(pl.multiple_of(g * 16 + 8, 8), 8), :] = dot(wt2[:, 128:256], d2.astype(BF))[8:16]

    def run(body, low, high):
        def step(i, carry):
            for u in range(U):
                body(low + i * U + u)
            return carry
        lax.fori_loop(0, (high - low) // U, step, 0)

    run(both, 0, EARLY)
    run(value_keep, EARLY, EARLY + KEPT)
    if EARLY + KEPT < 27:
        run(value, EARLY + KEPT, 27)

    r, c = iota((162, 432), 0), iota((162, 432), 1)
    first, place = lax.shift_right_logical(c, 4) * 6, c & 15
    pick_s = ones_where((r == first + place) & (place < 6))
    pick_r = ones_where((r == first + place - 8) & (place >= 8) & (place < 14))
    r, c = iota((96, 81), 0), iota((96, 81), 1)
    lane = r & 31
    grad_op = dot_nt(ones_where((c == lax.shift_right_logical(r, 5) * 27 + lane) & (lane < 27)), grad_ref[...]).astype(BF)
    parts = []
    for k in range(0, n, 768):
        sl = slice(k, k + 768)
        stress = dot(pick_s, oo[:, sl].astype(BF)).astype(BF)
        s_ref[:, sl] = stress
        parts.append(dot(grad_op, stress).astype(BF).astype(F32))
    s_copy = pltpu.make_async_copy(s_ref, s_out, s_sem)
    s_copy.start()
    force = jnp.concatenate(parts, 1)
    place = pm_ref[1:2, :]
    high = pm_ref[0:1, :] * 8 + lax.shift_right_logical(place, 2)
    low = place & 3
    masked = jnp.concatenate(
        [jnp.where(low == l, force[a * 32:(a + 1) * 32], 0.0).astype(BF) for a in range(3) for l in range(4)], 0)
    for k in range(2):
        onehot = ones_where(iota((512, n), 0) + k * 512 == high)
        out = dot_nt(onehot, masked).astype(BF)
        for a in range(3):
            send[k * 64:(k + 1) * 64, a] = out[:, a * 128:(a + 1) * 128].reshape(64, 8, 128)

    if REMOTE:
        pl.semaphore_wait(barrier, devices - 1)
        own = pltpu.make_async_copy(send.at[me], recv_ref.at[me], own_sem)
        own.start()

        def push(k, carry):
            t = lax.rem(me + k, devices)
            pltpu.make_async_remote_copy(
                src_ref=send.at[t], dst_ref=recv_ref.at[me], send_sem=send_sem, recv_sem=recv_sem,
                device_id=(lax.div(t, nd), lax.rem(t, nd)), device_id_type=MESH).start()
            return carry

        lax.fori_loop(1, devices, push, 0)

    run(rate, EARLY, EARLY + KEPT)
    if EARLY + KEPT < 27:
        run(both, EARLY + KEPT, 27)
    for k in range(0, n, 768):
        sl = slice(k, k + 768)
        r_ref[:, sl] = dot(pick_r, oo[:, sl].astype(BF)).astype(BF)
    r_copy = pltpu.make_async_copy(r_ref, r_out, r_sem)
    r_copy.start()

    node_copy.wait()
    node = jnp.floor((nodes[0:1, :].astype(F32) + 0.5) * (1.0 / 3.0))
    along = jnp.floor((node + 0.5) * (1.0 / 513.0))
    across = (node - along * 513.0) * 0.5
    half = jnp.where(across >= 128.0, 1.0, 0.0)
    tile, lane = (along + half).astype(jnp.int32), (across - 128.0 * half).astype(jnp.int32)
    density = dens_ref[...].reshape(1, n)
    d1 = density.astype(BF).astype(F32)
    d2 = (density - d1).astype(BF).astype(F32)
    rows = jnp.concatenate(
        [bm_ref[0:1, :].astype(F32), bm_ref[1:2, :].astype(F32), d1, d2, density - d1 - d2, jnp.zeros((3, n), F32)], 0)
    tiles = n // 128
    spread = jnp.concatenate([jnp.where(tile == t, rows, 0.0) for t in range(tiles)], 0).astype(BF)
    sums = dot_nt(spread, ones_where(iota((128, n), 0) == lane))
    sorted_rows = jnp.concatenate([sums[t * 8:(t + 1) * 8] for t in range(tiles)], 1)
    place = sorted_rows[1:2]
    place_high = jnp.floor(place * 0.25)
    slot = (sorted_rows[0:1] * 8.0 + place_high).astype(jnp.int32)
    low = (place - 4.0 * place_high).astype(jnp.int32)
    for k in range(0, n, 768):
        sl = slice(k, k + 768)
        pick[:, sl] = ones_where(iota((1024, 768), 0) == slot[:, sl])

    own.wait()
    every = pltpu.make_async_remote_copy(
        src_ref=send.at[pl.ds(0, devices - 1)], dst_ref=recv_ref.at[pl.ds(0, devices - 1)],
        send_sem=send_sem, recv_sem=recv_sem, device_id=(b, d), device_id_type=MESH)
    every.wait_send()
    every.wait_recv()

    slots = jnp.concatenate([recv_ref[:, a].reshape(1024, 128) for a in range(3)], 1)
    line = iota((32, 768), 0)

    def take(k):
        sl = slice(k, k + 768)
        found = lax.dot_general(slots, pick[:, sl], (((0,), (0,)), ((), ())), preferred_element_type=F32)
        for a in range(3):
            total = jnp.where(line == 27, sorted_rows[2 + a:3 + a, sl], 0.0)
            for l in range(4):
                total = total + jnp.where(low[:, sl] == l, found[a * 128 + l * 32:a * 128 + (l + 1) * 32], 0.0)
            grid_ref[a * 32:(a + 1) * 32, sl] = total.astype(BF)

    to_right = pltpu.make_async_remote_copy(
        src_ref=grid_ref.at[:, pl.ds(n - 768, 768)], dst_ref=left_ref, send_sem=right_send, recv_sem=left_recv,
        device_id=(b, lax.rem(d + 1, nd)), device_id_type=MESH)
    to_left = pltpu.make_async_remote_copy(
        src_ref=grid_ref.at[:, pl.ds(0, 768)], dst_ref=right_ref, send_sem=left_send, recv_sem=right_recv,
        device_id=(b, lax.rem(d + nd - 1, nd)), device_id_type=MESH)
    not_first, not_last = d > 0, d < nd - 1
    take(0)
    pl.when(not_first)(to_left.start)
    take(n - 768)
    pl.when(not_last)(to_right.start)
    for k in range(768, n - 768, 768):
        take(k)
    s_copy.wait()
    r_copy.wait()

    @pl.when(not_first)
    def _():
        to_left.wait_send()
        to_right.wait_recv()

    @pl.when(not_last)
    def _():
        to_right.wait_send()
        to_left.wait_recv()

    @pl.when(d == 0)
    def _():
        left_ref[...] = jnp.zeros((96, 768), BF)

    @pl.when(d == nd - 1)
    def _():
        right_ref[...] = jnp.zeros((96, 768), BF)


def pointwise(strain, rate, part_map, brick_map, connectivity, density, weight_in, bias_in, weight_mid, bias_mid, weight_out,
              grad_operator):
    n = strain.shape[1]
    row = lambda a: a.reshape(1, 128)
    points = jax.ShapeDtypeStruct((162, n), BF)
    halo = jax.ShapeDtypeStruct((96, 768), BF)
    vmem = pl.BlockSpec(memory_space=pltpu.VMEM)
    anywhere = pl.BlockSpec(memory_space=pl.ANY)
    return pl.pallas_call(
        pointwise_kernel,
        out_shape=(points, points, jax.ShapeDtypeStruct((96, n), BF), halo, halo),
        in_specs=[anywhere] * 2 + [vmem] * 2 + [anywhere] + [vmem] * 7,
        out_specs=(anywhere,) * 2 + (vmem,) * 3,
        scratch_shapes=[
            pltpu.VMEM((162, n), BF), pltpu.VMEM((162, n), BF), pltpu.VMEM((8, n), jnp.int32),
            pltpu.VMEM((432, n), BF), pltpu.VMEM((432, n), F32), pltpu.VMEM((3, 128, 128), F32), pltpu.VMEM((256, 16), BF),
            pltpu.VMEM((256, 256), BF), pltpu.VMEM((256, 256), BF), pltpu.VMEM((16, 256), BF), pltpu.VMEM((128, 3, 8, 128), BF),
            pltpu.VMEM((128, 3, 8, 128), BF), pltpu.VMEM((1024, n), BF), pltpu.VMEM((KEPT, 128, n), F32), pltpu.VMEM((KEPT, 2, 128, n), BF),
        ] + [pltpu.SemaphoreType.DMA] * 12,
        compiler_params=pltpu.CompilerParams(vmem_limit_bytes=60 << 20, collective_id=0, has_side_effects=True),
        name="pointwise",
    )(strain, rate, part_map, brick_map, connectivity, density, weight_in.T, row(bias_in), weight_mid, row(bias_mid), row(weight_out),
      grad_operator.T)

def fe_consts():
    m=np.array([[2,1,0],[1,4,1],[0,1,2]],np.float64)
    def rowof(u,w,z,d): return (u*3+w)*16+z*3+d
    A=np.zeros((144,144)); S=np.zeros((144,96)); dg=np.ones((144,1)); Q=np.zeros((216,144))
    for u in range(3):
     for w in range(3):
      for z in range(3):
       for d in range(3):
        r=rowof(u,w,z,d)
        S[r,d*32+(u*3+w)*3+z]=1
        dg[r]=m[u,u]*m[w,w]*m[z,z]
        Q[((u*3+w)*3+z)*8+d,r]=1
        for u2 in range(3):
         for w2 in range(3):
          for z2 in range(3):
            A[r,rowof(u2,w2,z2,d)]=m[u,u2]*m[w,w2]*m[z,z2]
    nn=np.arange(768); j=nn//3; z=nn%3; src=((j%2)*3+z)*128+j//2
    return A,S,np.tile(dg,(1,128)),Q,src[None,:].astype(np.int32)

def kernelE(s_in,r_in,L,O,Rt,A,S,dg,Q,src,s_out,r_out,out_ref,s_hold,r_hold,s_sem,r_sem):
    load_s=pltpu.make_async_copy(s_in,s_hold,s_sem); load_r=pltpu.make_async_copy(r_in,r_hold,r_sem)
    load_s.start(); load_r.start()
    s_copy=pltpu.make_async_copy(s_hold,s_out,s_sem); r_copy=pltpu.make_async_copy(r_hold,r_out,r_sem)
    ext=jnp.concatenate([L[...],O[...],Rt[...]],1)
    dens=(ext[27:28].astype(F32)+ext[59:60].astype(F32)+ext[91:92].astype(F32))*(1.0/216.0)
    def shl(x):
        n=x.shape[1]; y=pltpu.roll(x,n-1,1)
        i=lax.broadcasted_iota(jnp.int32,(1,n),1)&255
        return jnp.where(i==255,0.0,y)
    def shr(x):
        n=x.shape[1]; y=pltpu.roll(x,1,1)
        i=lax.broadcasted_iota(jnp.int32,(1,n),1)&255
        return jnp.where(i==0,0.0,y)
    def assemble(h):
        g=[h[16*q:16*q+16] for q in range(9)]
        for u in range(3):
            a0,a2=g[u*3],g[u*3+2]
            g[u*3]=a0+shr(a2); g[u*3+2]=a2+shl(a0)
        z=jnp.zeros((16,256),F32); n=h.shape[1]
        for w in range(3):
            b0,b2=g[w],g[6+w]
            g[w]=b0+jnp.concatenate([z,b2[:,:n-256]],1)
            g[6+w]=b2+jnp.concatenate([b0[:,256:],z],1)
        return jnp.concatenate(g,0)
    load=assemble(dot(S[...],ext))
    diag=assemble(dg[:,0:1]*dens)
    hinv=0.5/jnp.where(diag>0.0,diag,1.0)
    c=lambda x: x[:,256:x.shape[1]-256]
    load=c(load); hinv=c(hinv); dens=c(dens)
    load_s.wait(); load_r.wait()
    s_copy.start(); r_copy.start()
    f=load*hinv
    for it in range(2):
        fh=f.astype(BF); fl=(f-fh.astype(F32)).astype(BF)
        h=(dot(A[...],fh)+dot(A[...],fl))*dens
        s=assemble(h)
        f=c(f+(load-s)*hinv)
        load=c(load); hinv=c(hinv); dens=c(dens)
    fh=f.astype(BF); fl=(f-fh.astype(F32)).astype(BF)
    parts=[dot(Q[...],fh),dot(Q[...],fl)]
    P=jnp.where(lax.broadcasted_iota(jnp.int32,(768,768),0)==src[...],1.0,0.0).astype(BF)
    lhs=[]
    for half in range(2):
        for p in parts:
            rows=[]
            for i in range(19):
                u,ex=(i%2,i//2) if i<18 else (2,8)
                b=ex*256+half*128
                rows.append(jnp.concatenate([p[((u*3+w)*3+z)*8:((u*3+w)*3+z)*8+8,b:b+128] for w in range(2) for z in range(3)],1))
            lhs.append(jnp.concatenate(rows,0))
    Y=dot(jnp.concatenate(lhs,0).astype(BF),P)
    fs=parts[0]+parts[1]
    for i in range(19):
        u,ex=(i%2,i//2) if i<18 else (2,8)
        r=slice(8*i,8*i+8)
        h0=Y[0:152][r]+Y[152:304][r]; h1=Y[304:456][r]+Y[456:608][r]
        last=[fs[((u*3+2)*3+z)*8:((u*3+2)*3+z)*8+8,ex*256+255:ex*256+256] for z in range(3)]
        val=jnp.concatenate([h0,h1]+last,1)
        out_ref[:,i*1539:(i+1)*1539]=val[0:3]
    s_copy.wait(); r_copy.wait()

def callE(s,r,L,O,Rt):
    A,S,dg,Q,src=fe_consts()
    ops=[s,r,L,O,Rt,jnp.asarray(A,BF),jnp.asarray(S,BF),jnp.asarray(dg,F32),jnp.asarray(Q,BF),jnp.asarray(src)]
    vmem=pl.BlockSpec(memory_space=pltpu.VMEM); anywhere=pl.BlockSpec(memory_space=pl.ANY)
    point=jax.ShapeDtypeStruct(s.shape,BF)
    return pl.pallas_call(kernelE,out_shape=(point,point,jax.ShapeDtypeStruct((3,29241),F32)),
      in_specs=[anywhere]*2+[vmem]*(len(ops)-2),out_specs=(anywhere,anywhere,vmem),
      scratch_shapes=[pltpu.VMEM(s.shape,BF)]*2+[pltpu.SemaphoreType.DMA]*2,
      compiler_params=pltpu.CompilerParams(vmem_limit_bytes=60<<20),name="project")(*ops)


def per_device(*arguments):
    stress, stress_rate, grid, left, right = pointwise(*arguments)
    return callE(stress, stress_rate, left, grid, right)


def solution(mesh):
    split = P(None, ("brick", "dom"))
    return jax.shard_map(
        per_device,
        mesh=mesh,
        in_specs=(split,) * 5 + (P(("brick", "dom")),) + (P(),) * 6,
        out_specs=(split,) * 3,
        check_vma=False,
    )
```

```python
import functools

import jax
import jax.numpy as jnp
import numpy as np
from jax import lax
from jax.experimental import pallas as pl
from jax.experimental.pallas import tpu as pltpu
from jax.sharding import PartitionSpec as P

BF=jnp.bfloat16; F32=jnp.float32
def dot(a,b): return jnp.dot(a,b,preferred_element_type=F32)
def dot_nt(a,b): return lax.dot_general(a,b,(((1,),(1,)),((),())),preferred_element_type=F32)
MESH=pl.DeviceIdType.MESH
EARLY=12
KEPT=15
U=3
REMOTE=True


def iota(shape, axis):
    return lax.broadcasted_iota(jnp.int32, shape, axis)


def ones_where(mask):
    return jnp.where(mask, 1.0, 0.0).astype(BF)


def pointwise_kernel(x_ref, v_ref, pm_ref, bm_ref, conn_ref, dens_ref, win_ref, bin_ref, wmid_ref, bmid_ref, wout_ref, grad_ref,
                     s_out, r_out, grid_ref, left_ref, right_ref, s_ref, r_ref, nodes, x16, oo, bias, win2, wmid2, wback2, wt2, send,
                     recv_ref, pick, kept_act, kept, send_sem, recv_sem, own_sem, s_sem, r_sem, left_send, left_recv, right_send, right_recv,
                     x_sem, v_sem, node_sem):
    n = x_ref.shape[1]
    x_copy = pltpu.make_async_copy(x_ref, s_ref, x_sem)
    v_copy = pltpu.make_async_copy(v_ref, r_ref, v_sem)
    node_copy = pltpu.make_async_copy(conn_ref.at[pl.ds(0, 8)], nodes, node_sem)
    x_copy.start()
    v_copy.start()
    node_copy.start()
    if REMOTE:
        nb, nd = lax.axis_size("brick"), lax.axis_size("dom")
        devices = nb * nd
        b, d = lax.axis_index("brick"), lax.axis_index("dom")
        me = b * nd + d
        barrier = pltpu.get_barrier_semaphore()

        def greet(k, carry):
            t = lax.rem(me + k, devices)
            pl.semaphore_signal(barrier, inc=1, device_id=(lax.div(t, nd), lax.rem(t, nd)), device_id_type=MESH)
            return carry

        lax.fori_loop(1, devices, greet, 0)

    win = win_ref[...].astype(F32).T.astype(BF)
    e16 = lambda k: ones_where(iota((6, 16), 1) == iota((6, 16), 0) + k)
    win2[0:128] = dot(win, e16(0)).astype(BF)
    win2[128:256] = dot(win, e16(8)).astype(BF)
    wmid = wmid_ref[...]
    zero = jnp.zeros((128, 128), BF)
    wmid2[...] = jnp.concatenate([jnp.concatenate([wmid, zero], 1), jnp.concatenate([zero, wmid], 1)], 0)
    back = wmid.astype(F32).T.astype(BF)
    wback2[...] = jnp.concatenate([jnp.concatenate([back, zero], 1), jnp.concatenate([zero, back], 1)], 0)
    e = lambda k: ones_where(iota((16, 6), 0) == iota((16, 6), 1) + k)
    wt2[...] = jnp.concatenate([dot_nt(e(0), win).astype(BF), (-2.0 * dot_nt(e(8), win)).astype(BF)], 1)
    for k, row in enumerate((bin_ref, bmid_ref, wout_ref)):
        bias[k] = jnp.broadcast_to(row[...], (128, 128)).T

    r, c = iota((432, 162), 0), iota((432, 162), 1)
    first, place = lax.shift_right_logical(r, 4) * 6, r & 15
    selx = ones_where((c == first + place) & (place < 6))
    selv = ones_where((c == first + place - 8) & (place >= 8) & (place < 14))
    x_copy.wait()
    v_copy.wait()
    for k in range(0, n, 768):
        sl = slice(k, k + 768)
        x16[:, sl] = (dot(selx, s_ref[:, sl]) + dot(selv, r_ref[:, sl])).astype(BF)

    def column(k):
        return jnp.concatenate([bias[k]] * (n // 128), 1)

    def group(g):
        return pl.ds(pl.multiple_of(g * 16, 16), 16)

    def both(g):
        h = dot(win2[...], x16[group(g), :])
        act = jnp.tanh(h[:128] + column(0))
        slope = 1.0 - act * act
        tan = slope * h[128:]
        m = dot(wmid2[...], jnp.concatenate([act.astype(BF), tan.astype(BF)], 0))
        act2 = jnp.tanh(m[:128] + column(1))
        grad = column(2) * (1.0 - act2 * act2)
        bk = dot(wback2[...], jnp.concatenate([grad.astype(BF), (act2 * grad * m[128:]).astype(BF)], 0))
        b1 = bk[:128]
        d2 = slope * bk[128:] + act * tan * b1
        oo[group(g), :] = dot(wt2[...], jnp.concatenate([(slope * b1).astype(BF), d2.astype(BF)], 0))

    def value(g):
        act = jnp.tanh(dot(win2[0:128], x16[group(g), :]) + column(0))
        act2 = jnp.tanh(dot(wmid2[0:128, 0:128], act.astype(BF)) + column(1))
        grad = column(2) * (1.0 - act2 * act2)
        b1 = dot(wback2[0:128, 0:128], grad.astype(BF))
        oo[group(g), :] = dot(wt2[:, 0:128], ((1.0 - act * act) * b1).astype(BF))

    def value_keep(g):
        act = jnp.tanh(dot(win2[0:128], x16[group(g), :]) + column(0))
        act2 = jnp.tanh(dot(wmid2[0:128, 0:128], act.astype(BF)) + column(1))
        grad = column(2) * (1.0 - act2 * act2)
        b1 = dot(wback2[0:128, 0:128], grad.astype(BF))
        oo[group(g), :] = dot(wt2[:, 0:128], ((1.0 - act * act) * b1).astype(BF))
        kept_act[g - EARLY] = act
        kept[g - EARLY, 0] = (act2 * grad).astype(BF)
        kept[g - EARLY, 1] = b1.astype(BF)

    def rate(g):
        act = kept_act[g - EARLY]
        slope = 1.0 - act * act
        tan = slope * dot(win2[128:256], x16[group(g), :])
        curv = kept[g - EARLY, 0].astype(F32) * dot(wmid2[0:128, 0:128], tan.astype(BF))
        b2 = dot(wback2[0:128, 0:128], curv.astype(BF))
        d2 = slope * b2 + act * tan * kept[g - EARLY, 1].astype(F32)
        oo[pl.ds(pl.multiple_of(g * 16 + 8, 8), 8), :] = dot(wt2[:, 128:256], d2.astype(BF))[8:16]

    def run(body, low, high):
        def step(i, carry):
            for u in range(U):
                body(low + i * U + u)
            return carry
        lax.fori_loop(0, (high - low) // U, step, 0)

    run(both, 0, EARLY)
    run(value_keep, EARLY, EARLY + KEPT)
    if EARLY + KEPT < 27:
        run(value, EARLY + KEPT, 27)

    r, c = iota((162, 432), 0), iota((162, 432), 1)
    first, place = lax.shift_right_logical(c, 4) * 6, c & 15
    pick_s = ones_where((r == first + place) & (place < 6))
    pick_r = ones_where((r == first + place - 8) & (place >= 8) & (place < 14))
    r, c = iota((96, 81), 0), iota((96, 81), 1)
    lane = r & 31
    grad_op = dot_nt(ones_where((c == lax.shift_right_logical(r, 5) * 27 + lane) & (lane < 27)), grad_ref[...]).astype(BF)
    parts = []
    for k in range(0, n, 768):
        sl = slice(k, k + 768)
        stress = dot(pick_s, oo[:, sl].astype(BF)).astype(BF)
        s_ref[:, sl] = stress
        parts.append(dot(grad_op, stress).astype(BF).astype(F32))
    s_copy = pltpu.make_async_copy(s_ref, s_out, s_sem)
    s_copy.start()
    force = jnp.concatenate(parts, 1)
    place = pm_ref[1:2, :]
    high = pm_ref[0:1, :] * 8 + lax.shift_right_logical(place, 2)
    low = place & 3
    masked = jnp.concatenate(
        [jnp.where(low == l, force[a * 32:(a + 1) * 32], 0.0).astype(BF) for a in range(3) for l in range(4)], 0)
    for k in range(2):
        onehot = ones_where(iota((512, n), 0) + k * 512 == high)
        out = dot_nt(onehot, masked).astype(BF)
        for a in range(3):
            send[k * 64:(k + 1) * 64, a] = out[:, a * 128:(a + 1) * 128].reshape(64, 8, 128)

    if REMOTE:
        pl.semaphore_wait(barrier, devices - 1)
        own = pltpu.make_async_copy(send.at[me], recv_ref.at[me], own_sem)
        own.start()

        def push(k, carry):
            t = lax.rem(me + k, devices)
            pltpu.make_async_remote_copy(
                src_ref=send.at[t], dst_ref=recv_ref.at[me], send_sem=send_sem, recv_sem=recv_sem,
                device_id=(lax.div(t, nd), lax.rem(t, nd)), device_id_type=MESH).start()
            return carry

        lax.fori_loop(1, devices, push, 0)

    run(rate, EARLY, EARLY + KEPT)
    if EARLY + KEPT < 27:
        run(both, EARLY + KEPT, 27)
    for k in range(0, n, 768):
        sl = slice(k, k + 768)
        r_ref[:, sl] = dot(pick_r, oo[:, sl].astype(BF)).astype(BF)
    r_copy = pltpu.make_async_copy(r_ref, r_out, r_sem)
    r_copy.start()

    node_copy.wait()
    node = jnp.floor((nodes[0:1, :].astype(F32) + 0.5) * (1.0 / 3.0))
    along = jnp.floor((node + 0.5) * (1.0 / 513.0))
    across = (node - along * 513.0) * 0.5
    half = jnp.where(across >= 128.0, 1.0, 0.0)
    tile, lane = (along + half).astype(jnp.int32), (across - 128.0 * half).astype(jnp.int32)
    density = dens_ref[...].reshape(1, n)
    d1 = density.astype(BF).astype(F32)
    d2 = (density - d1).astype(BF).astype(F32)
    rows = jnp.concatenate(
        [bm_ref[0:1, :].astype(F32), bm_ref[1:2, :].astype(F32), d1, d2, density - d1 - d2, jnp.zeros((3, n), F32)], 0)
    tiles = n // 128
    spread = jnp.concatenate([jnp.where(tile == t, rows, 0.0) for t in range(tiles)], 0).astype(BF)
    sums = dot_nt(spread, ones_where(iota((128, n), 0) == lane))
    sorted_rows = jnp.concatenate([sums[t * 8:(t + 1) * 8] for t in range(tiles)], 1)
    place = sorted_rows[1:2]
    place_high = jnp.floor(place * 0.25)
    slot = (sorted_rows[0:1] * 8.0 + place_high).astype(jnp.int32)
    low = (place - 4.0 * place_high).astype(jnp.int32)
    for k in range(0, n, 768):
        sl = slice(k, k + 768)
        pick[:, sl] = ones_where(iota((1024, 768), 0) == slot[:, sl])

    own.wait()
    every = pltpu.make_async_remote_copy(
        src_ref=send.at[pl.ds(0, devices - 1)], dst_ref=recv_ref.at[pl.ds(0, devices - 1)],
        send_sem=send_sem, recv_sem=recv_sem, device_id=(b, d), device_id_type=MESH)
    every.wait_send()
    every.wait_recv()

    slots = jnp.concatenate([recv_ref[:, a].reshape(1024, 128) for a in range(3)], 1)
    line = iota((32, 768), 0)

    def take(k):
        sl = slice(k, k + 768)
        found = lax.dot_general(slots, pick[:, sl], (((0,), (0,)), ((), ())), preferred_element_type=F32)
        for a in range(3):
            total = jnp.where(line == 27, sorted_rows[2 + a:3 + a, sl], 0.0)
            for l in range(4):
                total = total + jnp.where(low[:, sl] == l, found[a * 128 + l * 32:a * 128 + (l + 1) * 32], 0.0)
            grid_ref[a * 32:(a + 1) * 32, sl] = total.astype(BF)

    to_right = pltpu.make_async_remote_copy(
        src_ref=grid_ref.at[:, pl.ds(n - 768, 768)], dst_ref=left_ref, send_sem=right_send, recv_sem=left_recv,
        device_id=(b, lax.rem(d + 1, nd)), device_id_type=MESH)
    to_left = pltpu.make_async_remote_copy(
        src_ref=grid_ref.at[:, pl.ds(0, 768)], dst_ref=right_ref, send_sem=left_send, recv_sem=right_recv,
        device_id=(b, lax.rem(d + nd - 1, nd)), device_id_type=MESH)
    not_first, not_last = d > 0, d < nd - 1
    take(0)
    pl.when(not_first)(to_left.start)
    take(n - 768)
    pl.when(not_last)(to_right.start)
    for k in range(768, n - 768, 768):
        take(k)
    s_copy.wait()
    r_copy.wait()

    @pl.when(not_first)
    def _():
        to_left.wait_send()
        to_right.wait_recv()

    @pl.when(not_last)
    def _():
        to_right.wait_send()
        to_left.wait_recv()

    @pl.when(d == 0)
    def _():
        left_ref[...] = jnp.zeros((96, 768), BF)

    @pl.when(d == nd - 1)
    def _():
        right_ref[...] = jnp.zeros((96, 768), BF)


def pointwise(strain, rate, part_map, brick_map, connectivity, density, weight_in, bias_in, weight_mid, bias_mid, weight_out,
              grad_operator):
    n = strain.shape[1]
    row = lambda a: a.reshape(1, 128)
    points = jax.ShapeDtypeStruct((162, n), BF)
    halo = jax.ShapeDtypeStruct((96, 768), BF)
    vmem = pl.BlockSpec(memory_space=pltpu.VMEM)
    anywhere = pl.BlockSpec(memory_space=pl.ANY)
    return pl.pallas_call(
        pointwise_kernel,
        out_shape=(points, points, jax.ShapeDtypeStruct((96, n), BF), halo, halo),
        in_specs=[anywhere] * 2 + [vmem] * 2 + [anywhere] + [vmem] * 7,
        out_specs=(anywhere,) * 2 + (vmem,) * 3,
        scratch_shapes=[
            pltpu.VMEM((162, n), BF), pltpu.VMEM((162, n), BF), pltpu.VMEM((8, n), jnp.int32),
            pltpu.VMEM((432, n), BF), pltpu.VMEM((432, n), F32), pltpu.VMEM((3, 128, 128), F32), pltpu.VMEM((256, 16), BF),
            pltpu.VMEM((256, 256), BF), pltpu.VMEM((256, 256), BF), pltpu.VMEM((16, 256), BF), pltpu.VMEM((128, 3, 8, 128), BF),
            pltpu.VMEM((128, 3, 8, 128), BF), pltpu.VMEM((1024, n), BF), pltpu.VMEM((KEPT, 128, n), F32), pltpu.VMEM((KEPT, 2, 128, n), BF),
        ] + [pltpu.SemaphoreType.DMA] * 12,
        compiler_params=pltpu.CompilerParams(vmem_limit_bytes=60 << 20, collective_id=0, has_side_effects=True),
        name="pointwise",
    )(strain, rate, part_map, brick_map, connectivity, density, weight_in.T, row(bias_in), weight_mid, row(bias_mid), row(weight_out),
      grad_operator.T)

def fe_consts():
    m=np.array([[2,1,0],[1,4,1],[0,1,2]],np.float64)
    def rowof(u,w,z,d): return (u*3+w)*16+z*3+d
    A=np.zeros((144,144)); S=np.zeros((144,96)); dg=np.ones((144,1)); Q=np.zeros((216,144))
    for u in range(3):
     for w in range(3):
      for z in range(3):
       for d in range(3):
        r=rowof(u,w,z,d)
        S[r,d*32+(u*3+w)*3+z]=1
        dg[r]=m[u,u]*m[w,w]*m[z,z]
        Q[((u*3+w)*3+z)*8+d,r]=1
        for u2 in range(3):
         for w2 in range(3):
          for z2 in range(3):
            A[r,rowof(u2,w2,z2,d)]=m[u,u2]*m[w,w2]*m[z,z2]
    nn=np.arange(768); j=nn//3; z=nn%3; src=((j%2)*3+z)*128+j//2
    return A,S,np.tile(dg,(1,128)),Q,src[None,:].astype(np.int32)

def kernelE(s_in,r_in,L,O,Rt,A,S,dg,Q,src,s_out,r_out,out_ref,s_hold,r_hold,s_sem,r_sem):
    load_s=pltpu.make_async_copy(s_in,s_hold,s_sem); load_r=pltpu.make_async_copy(r_in,r_hold,r_sem)
    load_s.start(); load_r.start()
    s_copy=pltpu.make_async_copy(s_hold,s_out,s_sem); r_copy=pltpu.make_async_copy(r_hold,r_out,r_sem)
    ext=jnp.concatenate([L[...],O[...],Rt[...]],1)
    dens=(ext[27:28].astype(F32)+ext[59:60].astype(F32)+ext[91:92].astype(F32))*(1.0/216.0)
    def shl(x):
        n=x.shape[1]; y=pltpu.roll(x,n-1,1)
        i=lax.broadcasted_iota(jnp.int32,(1,n),1)&255
        return jnp.where(i==255,0.0,y)
    def shr(x):
        n=x.shape[1]; y=pltpu.roll(x,1,1)
        i=lax.broadcasted_iota(jnp.int32,(1,n),1)&255
        return jnp.where(i==0,0.0,y)
    def assemble(h):
        g=[h[16*q:16*q+16] for q in range(9)]
        for u in range(3):
            a0,a2=g[u*3],g[u*3+2]
            g[u*3]=a0+shr(a2); g[u*3+2]=a2+shl(a0)
        z=jnp.zeros((16,256),F32); n=h.shape[1]
        for w in range(3):
            b0,b2=g[w],g[6+w]
            g[w]=b0+jnp.concatenate([z,b2[:,:n-256]],1)
            g[6+w]=b2+jnp.concatenate([b0[:,256:],z],1)
        return jnp.concatenate(g,0)
    load=assemble(dot(S[...],ext))
    diag=assemble(dg[:,0:1]*dens)
    hinv=0.5/jnp.where(diag>0.0,diag,1.0)
    c=lambda x: x[:,256:x.shape[1]-256]
    load=c(load); hinv=c(hinv); dens=c(dens)
    load_s.wait(); load_r.wait()
    s_copy.start(); r_copy.start()
    f=load*hinv
    for it in range(2):
        fh=f.astype(BF); fl=(f-fh.astype(F32)).astype(BF)
        h=(dot(A[...],fh)+dot(A[...],fl))*dens
        s=assemble(h)
        f=c(f+(load-s)*hinv)
        load=c(load); hinv=c(hinv); dens=c(dens)
    fh=f.astype(BF); fl=(f-fh.astype(F32)).astype(BF)
    parts=[dot(Q[...],fh),dot(Q[...],fl)]
    P=jnp.where(lax.broadcasted_iota(jnp.int32,(768,768),0)==src[...],1.0,0.0).astype(BF)
    lhs=[]
    for half in range(2):
        for p in parts:
            rows=[]
            for i in range(19):
                u,ex=(i%2,i//2) if i<18 else (2,8)
                b=ex*256+half*128
                rows.append(jnp.concatenate([p[((u*3+w)*3+z)*8:((u*3+w)*3+z)*8+8,b:b+128] for w in range(2) for z in range(3)],1))
            lhs.append(jnp.concatenate(rows,0))
    Y=dot(jnp.concatenate(lhs,0).astype(BF),P)
    fs=parts[0]+parts[1]
    for i in range(19):
        u,ex=(i%2,i//2) if i<18 else (2,8)
        r=slice(8*i,8*i+8)
        h0=Y[0:152][r]+Y[152:304][r]; h1=Y[304:456][r]+Y[456:608][r]
        last=[fs[((u*3+2)*3+z)*8:((u*3+2)*3+z)*8+8,ex*256+255:ex*256+256] for z in range(3)]
        val=jnp.concatenate([h0,h1]+last,1)
        out_ref[:,i*1539:(i+1)*1539]=val[0:3]
    s_copy.wait(); r_copy.wait()

def callE(s,r,L,O,Rt):
    A,S,dg,Q,src=fe_consts()
    ops=[s,r,L,O,Rt,jnp.asarray(A,BF),jnp.asarray(S,BF),jnp.asarray(dg,F32),jnp.asarray(Q,BF),jnp.asarray(src)]
    vmem=pl.BlockSpec(memory_space=pltpu.VMEM); anywhere=pl.BlockSpec(memory_space=pl.ANY)
    point=jax.ShapeDtypeStruct(s.shape,BF)
    return pl.pallas_call(kernelE,out_shape=(point,point,jax.ShapeDtypeStruct((3,29241),F32)),
      in_specs=[anywhere]*2+[vmem]*(len(ops)-2),out_specs=(anywhere,anywhere,vmem),
      scratch_shapes=[pltpu.VMEM(s.shape,BF)]*2+[pltpu.SemaphoreType.DMA]*2,
      compiler_params=pltpu.CompilerParams(vmem_limit_bytes=60<<20),name="project")(*ops)


def per_device(*arguments):
    stress, stress_rate, grid, left, right = pointwise(*arguments)
    return callE(stress, stress_rate, left, grid, right)


def solution(mesh):
    split = P(None, ("brick", "dom"))
    return jax.shard_map(
        per_device,
        mesh=mesh,
        in_specs=(split,) * 5 + (P(("brick", "dom")),) + (P(),) * 6,
        out_specs=(split,) * 3,
        check_vma=False,
    )
```
